256 devices in a mesh: tm: 8 (over z_hi, y), space: 32 (over z_lo, x, core).
Axes of the slice: x: 4, y: 4, z: 8 (z_hi: 2, z_lo: 4; z = z_hi * 4 + z_lo), core: 2. Of those that a mesh axis runs over, the one named last changes fastest.
Arguments:
- slice_start: float32 [8, 64, 16, 4096], P('tm', None, None, 'space'), may hold values from -6 to 6
- volume: float32 [64, 64], replicated, may hold values from -0.75 to 0.75
- lift_matrix: float32 [64, 96], replicated, may hold values from -0.625 to 0.625
- element_rate: float32 [4096], P('space'), may hold values from 0.5 to 1.5
- position: int32 [4096], P('space'), may hold values from 0 to 127, as said below
- neighbours: int32 [4, 4096], P(None, 'space'), may hold values from 0 to 127, as said below
Outputs:
- slice_end: float32 [8, 64, 16, 4096], P('tm', None, None, 'space')
The draws below stay inside these ranges and needn't reach their ends.
Inputs may be any that keep to these rules, and one draw needn't show every extreme that they name: Within each device's 128 elements every position occurs exactly once. `neighbours`: rows 0, 1, 2, 3 name the local element (numbered within the device) whose position is one row before, one row after (modulo 8), one column before, one column after (modulo 16) that of element e.
All inputs are finite; a program needn't handle non-finite values.
Results may differ from the reference program's by a relative error of at most 0.0001.
Values sent between devices are 32-bit elements; how exact they have to be, the bound alone decides.
No kernel may reach another device: no remote copies, remote signals or barrier semaphores. Data moves between devices by JAX's collectives and lax.ppermute only.
A program may use at most 128 MiB of HBM per device.

```python
import math
import jax
import jax.numpy as jnp
from jax import lax

SOURCES = 16
NODES = 64
GY = 8
GZ = 16
ELEMS = 4096
SLICES = 8


def element_numbering(key):
    subkeys = jax.random.split(key, ELEMS // (GY * GZ))
    return jax.vmap(lambda subkey: jax.random.permutation(subkey, GY * GZ))(subkeys).astype(jnp.int32)


def draw_position(key, part):
    order = element_numbering(key)
    return order.reshape(-1).astype(jnp.int32)


def draw_neighbours(key, part):
    order = element_numbering(key)
    slot_of = jnp.argsort(order, axis=1, stable=True).astype(jnp.int32)
    row_index = order // GZ
    col_index = order % GZ

    def local_slot(row_value, col_value):
        place = row_value % GY * GZ + col_value % GZ
        return jnp.take_along_axis(slot_of, place.astype(jnp.int32), axis=1)
    stacked = jnp.stack([local_slot(row_index - 1, col_index), local_slot(row_index + 1, col_index), local_slot(row_index, col_index - 1), local_slot(row_index, col_index + 1)])
    return stacked.reshape(4, -1).astype(jnp.int32)


def block_levels(stream_key, shape, cuts, least, top_value):
    level, own = 1.0, jax.random.fold_in(stream_key, 6)
    for dim, blocks in cuts:
        draws = jnp.exp(jax.random.uniform(jax.random.fold_in(own, dim), (blocks,), jnp.float32, least / len(cuts), top_value / len(cuts)))
        level = level * jnp.repeat(draws, shape[dim] // blocks).reshape([-1 if axis == dim else 1 for axis in range(len(shape))])
    return level


def noise(rng, extent, scale, most, pieces=(), kind=jnp.bfloat16):
    factor_of = block_levels(rng, extent, pieces, -0.22, 0.18) if pieces else 1.0
    values = jax.random.normal(rng, extent, jnp.float32) * scale * factor_of
    return jnp.minimum(jnp.maximum(values, -most), most).astype(kind)


def setup_inputs(seed: int = 0) -> dict:
    streams_of = jax.random.split(jax.random.key(seed), 7)
    slice_start = noise(streams_of[0], (SLICES, NODES, SOURCES, ELEMS), 1.0, 6.0, ((0, 8), (3, 32)), jnp.float32)
    volume = noise(streams_of[1], (NODES, NODES), NODES ** -0.5, 0.75, (), jnp.float32)
    lift_matrix = noise(streams_of[2], (NODES, 96), 96 ** -0.5, 0.625, (), jnp.float32)
    element_rate = jnp.clip(jnp.exp(math.log(1.5) - 1.0986123 * jax.random.uniform(streams_of[3], (ELEMS,), jnp.float32) ** block_levels(streams_of[3], (ELEMS,), ((0, 32),), -0.2, 0.2)), 0.5, 1.5)
    position = draw_position(jax.random.fold_in(streams_of[6], 71), 0)
    neighbours = draw_neighbours(jax.random.fold_in(streams_of[6], 71), 0)
    return dict(slice_start=slice_start, volume=volume, lift_matrix=lift_matrix, element_rate=element_rate, position=position, neighbours=neighbours)


step_size = 0.25


def face_views(field):
    shape = field.shape
    cubes = field.reshape(4, 4, 4, shape[1], shape[2])
    picked = [cubes[0], cubes[3], cubes[:, 0], cubes[:, 3], cubes[:, :, 0], cubes[:, :, 3]]
    return [item.reshape(16, shape[1], shape[2]) for item in picked]


def global_links(position, neighbours):
    blocks = ELEMS // (GY * GZ)
    layer = GY * GZ
    places = position.reshape(blocks, layer)
    rows = jnp.arange(blocks, dtype=jnp.int32)[:, None]
    slot_of = jnp.zeros_like(places).at[rows, places].set(jnp.arange(layer, dtype=jnp.int32)[None, :])
    base = rows * layer
    minus_x = jnp.roll(base, 1, axis=0) + jnp.take_along_axis(jnp.roll(slot_of, 1, axis=0), places, axis=1)
    plus_x = jnp.roll(base, -1, axis=0) + jnp.take_along_axis(jnp.roll(slot_of, -1, axis=0), places, axis=1)
    others = neighbours.reshape(4, blocks, layer) + base[None]
    return jnp.concatenate([minus_x[None], plus_x[None], others], axis=0).reshape(6, -1).astype(jnp.int32)


def operate(field, element_rate, weights, links):
    faces = face_views(field)
    jumps = [jnp.take(faces[which ^ 1], links[which], axis=2) - faces[which] for which in range(6)]
    stacked = jnp.concatenate([field] + jumps, axis=0)
    mixed = jnp.dot(weights, stacked.reshape(stacked.shape[0], -1), precision=lax.Precision.HIGHEST, preferred_element_type=jnp.float32)
    return element_rate * mixed.reshape(field.shape) - field


def reference(slice_start, volume, lift_matrix, element_rate, position, neighbours):
    links = global_links(position, neighbours)
    weights = jnp.concatenate([volume, lift_matrix], axis=1)

    def apply_op(field):
        return operate(field, element_rate, weights, links)

    def coarse(field):
        return field + step_size * apply_op(field)

    def fine(field):
        first = apply_op(field)
        second = apply_op(field + 0.5 * step_size * first)
        third = apply_op(field + 0.5 * step_size * second)
        fourth = apply_op(field + step_size * third)
        return field + (step_size / 6.0) * (first + 2.0 * second + 2.0 * third + fourth)

    corrections = []
    for slice_index in range(SLICES):
        start_now = slice_start[slice_index]
        corrections.append(fine(start_now) - coarse(start_now))
    current = slice_start[0]
    results = []
    for slice_index in range(SLICES):
        current = coarse(current) + corrections[slice_index]
        results.append(current)
    return jnp.stack(results)
```

```python
import functools

import jax
import jax.numpy as jnp
import numpy as np
from jax import lax
from jax.experimental import pallas as pl
from jax.experimental.pallas import tpu as pltpu
from jax.sharding import Mesh, PartitionSpec as P

STEP = 0.25
NODES = 64
LANES = 128
SOURCES = 16
COLS = 16
BLOCK = 8
WIDE, NARROW = 7, 5
RANK = 192
VMEM = 40 * 1024 * 1024
F32 = jnp.float32


def selection():
    table = np.zeros((160, RANK), np.float32)
    for a in range(4):
        for b in range(4):
            for c in range(4):
                node = a * 16 + b * 4 + c
                table[node, node] += 1.0
                faces = ((a, 0, b * 4 + c), (b, 2, a * 4 + c), (c, 4, a * 4 + b))
                for place, low, rank in faces:
                    if place == 0:
                        table[64 + low * 16 + rank, node] -= 1.0
                    if place == 3:
                        table[64 + (low + 1) * 16 + rank, node] -= 1.0
                if c == 0:
                    table[64 + 5 * 16 + a * 4 + b, 128 + node] = 1.0
                if c == 3:
                    table[64 + 4 * 16 + a * 4 + b, 128 + node] = 1.0
    for k in range(16):
        table[64 + k, 64 + k] = 1.0
        table[64 + 16 + k, 80 + k] = 1.0
    for a in range(4):
        for c in range(4):
            table[64 + 3 * 16 + a * 4 + c, 96 + a * 8 + c] = 1.0
            table[64 + 2 * 16 + a * 4 + c, 96 + a * 8 + 4 + c] = 1.0
    return table


def gather_lanes(x, index):
    return jnp.take_along_axis(x, index, axis=1, mode="promise_in_bounds")


def neighbour_lanes():
    lane = lax.broadcasted_iota(jnp.int32, (8, LANES), 1)
    row = lax.broadcasted_iota(jnp.int32, (8, LANES), 0)
    y_index = jnp.where(row < 4, lane + COLS, lane + (LANES - COLS)) & (LANES - 1)
    col = lane & (COLS - 1)
    z_step = jnp.where((row & 3) == 0, 1, COLS - 1)
    z_index = (lane - col) + ((col + z_step) & (COLS - 1))
    return y_index, z_index, row < 4


def operand(before, here, after, lanes):
    y_index, z_index, low = lanes
    ys = [
        gather_lanes(jnp.where(low, here[16 * a : 16 * a + 8], here[16 * a + 8 : 16 * a + 16]), y_index)
        for a in range(4)
    ]
    zs = [gather_lanes(here[8 * k : 8 * k + 8], z_index) for k in range(8)]
    return jnp.concatenate([here, before[48:64], after[0:16]] + ys + zs, axis=0)


def split(x):
    high = x.astype(jnp.bfloat16)
    low = (x - high.astype(F32)).astype(jnp.bfloat16)
    return high, low


def product(weights, x):
    high, low = split(x)
    first = jnp.dot(weights, high, preferred_element_type=F32)
    second = jnp.dot(weights[:NODES], low, preferred_element_type=F32)
    return first[:NODES] + first[NODES:] + second


def stacked_weights(w_ref):
    high, low = split(w_ref[...])
    return jnp.concatenate([high, low], axis=0)


def sweep(count, load, rates, weights, lanes, store):
    def body(pair, carry):
        k = pair * 2
        v = [load(k + i) for i in range(4)]
        x = [operand(v[i], v[i + 1], v[i + 2], lanes) for i in range(2)]
        y = product(weights, jnp.concatenate(x, axis=1))
        for i in range(2):
            store(k + i, v[i + 1], rates(k + i) * y[:, i * LANES : (i + 1) * LANES])
        return carry

    lax.fori_loop(0, count // 2, body, 0, unroll=True)


def slot_row(position):
    where = lax.broadcasted_iota(jnp.int32, (LANES, LANES), 0)
    hit = jnp.where(position == where, 1.0, 0.0).astype(jnp.bfloat16)
    ids = lax.broadcasted_iota(jnp.int32, (16, LANES), 1).astype(F32).astype(jnp.bfloat16)
    found = lax.dot_general(ids, hit, (((1,), (1,)), ((), ())), preferred_element_type=F32)
    return found[0:1].astype(jnp.int32)


def pre_kernel(position_ref, rate_ref, field_ref, out_ref, rate_out_ref):
    index = jnp.broadcast_to(slot_row(position_ref[...]), (NODES, LANES))
    for s in range(SOURCES):
        out_ref[s] = gather_lanes(field_ref[pl.ds(s, NODES, stride=SOURCES), :], index)
    rate_out_ref[...] = gather_lanes(jnp.broadcast_to(rate_ref[...], (8, LANES)), index[:8])


def post_kernel(position_ref, field_ref, out_ref):
    index = jnp.broadcast_to(position_ref[...], (NODES, LANES))
    for s in range(SOURCES):
        out_ref[pl.ds(s, NODES, stride=SOURCES), :] = gather_lanes(field_ref[s], index)


def fine_kernel(flag_ref, w_ref, rate_ref, own_ref, left_ref, right_ref, out0_ref, out1_ref, u_ref, p_ref):
    weights = stacked_weights(w_ref)
    lanes = neighbour_lanes()
    takes_end = jnp.where(jnp.logical_and(flag_ref[0] == 0, flag_ref[1] == 0), 1.0, 0.0).astype(F32)
    for slot, (width, start) in enumerate(((WIDE, 0), (NARROW, WIDE))):
        size = BLOCK + 2 * width
        for k in range(width):
            u_ref[k] = left_ref[start + k]
            u_ref[width + BLOCK + k] = right_ref[start + k]
        for k in range(BLOCK):
            u_ref[width + k] = own_ref[slot, k]
        out = (out0_ref, out1_ref)[slot]

        for power in range(4):
            first = power + 1
            source = u_ref if power == 0 else p_ref.at[power - 1]

            def load(k, source=source, first=first):
                return source[first - 1 + k]

            def rates(k, first=first, width=width):
                return rate_ref[pl.ds(WIDE - width + first + k, 1), :]

            def store(k, v, y, power=power, first=first, slot=slot, out=out):
                p = y - v
                if power < 3:
                    p_ref[power, first + k] = p
                else:
                    total = (STEP**2 / 2) * p_ref[1, first + k] + (STEP**3 / 6) * v + (STEP**4 / 24) * p
                    if slot == 0:
                        total = total + takes_end * (u_ref[first + k] + STEP * p_ref[0, first + k])
                    out[k] = total

            sweep(size - 2 * first, load, rates, weights, lanes, store)


def advance_from(start, widths, corrections, rate_ref, weights, lanes, ends, work_ref):
    source, source_width = start
    for n, (width, (correction, correction_width)) in enumerate(zip(widths, corrections)):
        target = work_ref.at[n % 2]

        def load(k, source=source, skip=source_width - width - 1):
            return source[skip + k]

        def rates(k, width=width):
            return rate_ref[pl.ds(WIDE - width + k, 1), :]

        def store(k, v, y, n=n, width=width, correction=correction, skip=correction_width - width, target=target):
            value = (1.0 - STEP) * v + STEP * y + correction(skip + k)
            target[k] = value

        sweep(BLOCK + 2 * width, load, rates, weights, lanes, store)
        for k in range(BLOCK):
            ends(n, k, target[width + k])
        source, source_width = target, width


def picked(core, mine_ref, other_ref, owner):
    def read(k):
        return jnp.where(core == owner, mine_ref[k], other_ref[k])

    return read


def first_kernel(flag_ref, w_ref, rate_ref, mine0_ref, mine1_ref, other0_ref, other1_ref, end_ref, start_ref, work_ref):
    weights = stacked_weights(w_ref)
    lanes = neighbour_lanes()
    core = flag_ref[1]
    start = picked(core, mine0_ref, other0_ref, 0)
    for k in range(BLOCK + 6):
        start_ref[k] = start(k)
    for k in range(BLOCK):
        end_ref[0, k] = start_ref[3 + k]

    def ends(n, k, value):
        end_ref[n + 1, k] = value

    corrections = (
        (picked(core, mine0_ref, other0_ref, 1), 3),
        (picked(core, mine1_ref, other1_ref, 1), 1),
        (picked(core, mine1_ref, other1_ref, 0), 1),
    )
    advance_from((start_ref, 3), (2, 1, 0), corrections, rate_ref, weights, lanes, ends, work_ref)


def second_kernel(
    flag_ref, w_ref, rate_ref, mine0_ref, mine1_ref, other0_ref, other1_ref, end_ref, got_ref, back_ref,
    out_ref, start_ref, work_ref, late_ref,
):
    weights = stacked_weights(w_ref)
    lanes = neighbour_lanes()
    core = flag_ref[1]
    for k in range(4):
        start_ref[k] = jnp.where(core == 0, got_ref[k], back_ref[k])
        start_ref[4 + k] = jnp.where(core == 0, got_ref[4 + k], back_ref[4 + k])
        start_ref[8 + k] = jnp.where(core == 0, back_ref[4 + k], got_ref[4 + k])
        start_ref[12 + k] = jnp.where(core == 0, back_ref[k], got_ref[k])

    def ends(n, k, value):
        late_ref[n, k] = value

    corrections = (
        (picked(core, mine0_ref, other0_ref, 0), 3),
        (picked(core, mine0_ref, other0_ref, 1), 3),
        (picked(core, mine1_ref, other1_ref, 1), 1),
        (picked(core, mine1_ref, other1_ref, 0), 1),
    )
    advance_from((start_ref, 4), (3, 2, 1, 0), corrections, rate_ref, weights, lanes, ends, work_ref)
    early = flag_ref[0] == 0
    for n in range(4):
        for x in range(4):
            out_ref[n * 4 + x] = jnp.where(early, end_ref[n, 2 * x + core], late_ref[n, 2 * x + core])


def call(kernel, outs, scratch, n_in, flags=True):
    whole = pl.BlockSpec(memory_space=pltpu.VMEM)
    first = [pl.BlockSpec(memory_space=pltpu.SMEM)] if flags else []
    return pl.pallas_call(
        kernel,
        out_shape=tuple(jax.ShapeDtypeStruct(s, F32) for s in outs),
        in_specs=first + [whole] * (n_in - len(first)),
        out_specs=tuple(whole for _ in outs),
        scratch_shapes=[pltpu.VMEM(s, F32) for s in scratch],
        compiler_params=pltpu.CompilerParams(vmem_limit_bytes=VMEM),
    )


LAYER = (NODES, LANES)


def ring(size, step):
    return [(i, (i + step) % size) for i in range(size)]


def shards(slice_start, volume, lift_matrix, element_rate, position, neighbours):
    del neighbours
    zh, core, zl = lax.axis_index("zh"), lax.axis_index("c"), lax.axis_index("zl")
    flags = jnp.stack([zh, core]).astype(jnp.int32)
    weights = jnp.dot(
        jnp.concatenate([volume, lift_matrix], axis=1), jnp.asarray(selection()), precision=lax.Precision.HIGHEST
    )
    row = position.reshape(1, LANES)
    natural, rate = call(pre_kernel, ((SOURCES,) + LAYER, (8, LANES)), (), 3, False)(
        row, element_rate.reshape(1, LANES), slice_start.reshape(NODES * SOURCES, LANES)
    )
    all_rates = lax.all_gather(rate[0:1], ("zl", "x", "c"), axis=0, tiled=True)
    layers = all_rates.shape[0]
    rates = lax.dynamic_slice_in_dim(
        jnp.concatenate([all_rates] * 3, axis=0), layers + zl * BLOCK - WIDE, BLOCK + 2 * WIDE, axis=0
    )

    mixed = lax.all_to_all(natural, ("y", "x"), 0, 0, tiled=True).reshape((4, 4) + LAYER)
    outer, inner = jnp.stack([mixed[0], mixed[3]]), jnp.stack([mixed[1], mixed[2]])
    swap = [(0, 1), (1, 0)]
    received = lax.ppermute(jnp.where(core == 0, inner, outer), "c", swap)
    kept = jnp.where(core == 0, outer, inner)
    even, odd = jnp.where(core == 0, kept, received), jnp.where(core == 0, received, kept)
    own = jnp.stack([even, odd], axis=2).reshape((2, BLOCK) + LAYER)

    size = lax.axis_size("zl")
    left = lax.ppermute(
        jnp.concatenate([own[0, BLOCK - WIDE :], own[1, BLOCK - NARROW :]], axis=0), "zl", ring(size, 1)
    )
    right = lax.ppermute(jnp.concatenate([own[0, :WIDE], own[1, :NARROW]], axis=0), "zl", ring(size, -1))
    mine = call(
        fine_kernel,
        ((BLOCK + 6,) + LAYER, (BLOCK + 2,) + LAYER),
        ((BLOCK + 2 * WIDE,) + LAYER, (3, BLOCK + 2 * WIDE) + LAYER),
        6,
    )(flags, weights, rates, own, left, right)
    other = tuple(lax.ppermute(part, "c", swap) for part in mine)

    (ends,) = call(
        first_kernel, ((4, BLOCK) + LAYER,), ((BLOCK + 6,) + LAYER, (2, BLOCK + 6) + LAYER), 7
    )(flags, weights, rates, *mine, *other)

    last = ends[3]
    own_half = jnp.where(core == 0, last[:4], last[4:])
    halo_half = jnp.where(core == 0, last[4:], last[:4])
    straight = [(z * 2 + c, (4 + z) * 2 + c) for z in range(4) for c in range(2)]
    beside = [(z * 2 + c, (4 + (z + (1, -1)[c]) % 4) * 2 + c) for z in range(4) for c in range(2)]
    axes = ("zh", "zl", "c")
    got = jnp.concatenate([lax.ppermute(halo_half, axes, beside), lax.ppermute(own_half, axes, straight)], axis=0)
    back = lax.ppermute(got, "c", swap)
    (out,) = call(
        second_kernel,
        ((SOURCES,) + LAYER,),
        ((BLOCK + 8,) + LAYER, (2, BLOCK + 6) + LAYER, (4, BLOCK) + LAYER),
        10,
    )(flags, weights, rates, *mine, *other, ends, got, back)
    home = lax.all_to_all(out, ("y", "x"), 0, 0, tiled=True)
    (final,) = call(post_kernel, ((NODES * SOURCES, LANES),), (), 2, False)(row, home)
    return final.reshape(slice_start.shape)


def solution(mesh):
    fine_mesh = Mesh(mesh.devices.reshape(2, 4, 4, 4, 2), ("zh", "y", "zl", "x", "c"))
    tm, space = ("zh", "y"), ("zl", "x", "c")
    placed = (P(tm, None, None, space), P(), P(), P(space), P(space), P(None, space))
    return jax.shard_map(
        shards, mesh=fine_mesh, in_specs=placed, out_specs=P(tm, None, None, space), check_vma=False
    )
```

```python
import functools

import jax
import jax.numpy as jnp
import numpy as np
from jax import lax
from jax.experimental import pallas as pl
from jax.experimental.pallas import tpu as pltpu
from jax.sharding import Mesh, PartitionSpec as P

STEP = 0.25
NODES = 64
LANES = 128
SOURCES = 16
COLS = 16
BLOCK = 8
CHUNK = 72
TRACES = 19
FACE = 16
RANK = 192
VMEM = 40 * 1024 * 1024
F32 = jnp.float32


def selection():
    table = np.zeros((160, RANK), np.float32)
    for a in range(4):
        for b in range(4):
            for c in range(4):
                node = a * 16 + b * 4 + c
                table[node, node] += 1.0
                faces = ((a, 0, b * 4 + c), (b, 2, a * 4 + c), (c, 4, a * 4 + b))
                for place, low, rank in faces:
                    if place == 0:
                        table[64 + low * 16 + rank, node] -= 1.0
                    if place == 3:
                        table[64 + (low + 1) * 16 + rank, node] -= 1.0
                if c == 0:
                    table[64 + 5 * 16 + a * 4 + b, 128 + node] = 1.0
                if c == 3:
                    table[64 + 4 * 16 + a * 4 + b, 128 + node] = 1.0
    for k in range(16):
        table[64 + k, 64 + k] = 1.0
        table[64 + 16 + k, 80 + k] = 1.0
    for a in range(4):
        for c in range(4):
            table[64 + 3 * 16 + a * 4 + c, 96 + a * 8 + c] = 1.0
            table[64 + 2 * 16 + a * 4 + c, 96 + a * 8 + 4 + c] = 1.0
    return table


def gather_lanes(x, index):
    return jnp.take_along_axis(x, index, axis=1, mode="promise_in_bounds")


def neighbour_lanes():
    lane = lax.broadcasted_iota(jnp.int32, (8, LANES), 1)
    row = lax.broadcasted_iota(jnp.int32, (8, LANES), 0)
    y_index = jnp.where(row < 4, lane + COLS, lane + (LANES - COLS)) & (LANES - 1)
    col = lane & (COLS - 1)
    z_step = jnp.where((row & 3) == 0, 1, COLS - 1)
    z_index = (lane - col) + ((col + z_step) & (COLS - 1))
    return y_index, z_index, row < 4


def operand(before, here, after, lanes):
    y_index, z_index, low = lanes
    ys = [
        gather_lanes(jnp.where(low, here[16 * a : 16 * a + 8], here[16 * a + 8 : 16 * a + 16]), y_index)
        for a in range(4)
    ]
    zs = [gather_lanes(here[8 * k : 8 * k + 8], z_index) for k in range(8)]
    return jnp.concatenate([here, before, after] + ys + zs, axis=0)


def split(x):
    high = x.astype(jnp.bfloat16)
    low = (x - high.astype(F32)).astype(jnp.bfloat16)
    return high, low


def product(weights, x):
    high, low = split(x)
    first = jnp.dot(weights, high, preferred_element_type=F32)
    second = jnp.dot(weights[:NODES], low, preferred_element_type=F32)
    return first[:NODES] + first[NODES:] + second


def stacked_weights(w_ref):
    high, low = split(w_ref[...])
    return jnp.concatenate([high, low], axis=0)


def sweep(count, load, rates, weights, lanes, store, inject=None):
    for k in range(0, count, 2):
        v = [load(k + i) for i in range(4)]
        x = []
        for i in range(2):
            before, after = v[i][48:64], v[i + 2][0:16]
            extra = inject(k + i) if inject is not None else (None, None)
            before = before if extra[0] is None else before + extra[0]
            after = after if extra[1] is None else after + extra[1]
            x.append(operand(before, v[i + 1], after, lanes))
        y = product(weights, jnp.concatenate(x, axis=1))
        for i in range(2):
            rate = jnp.concatenate([rates(k + i)] * (NODES // 8), axis=0)
            store(k + i, v[i + 1], rate * y[:, i * LANES : (i + 1) * LANES])


def slot_row(position):
    where = lax.broadcasted_iota(jnp.int32, (LANES, LANES), 0)
    hit = jnp.where(position == where, 1.0, 0.0).astype(jnp.bfloat16)
    ids = lax.broadcasted_iota(jnp.int32, (16, LANES), 1).astype(F32).astype(jnp.bfloat16)
    found = lax.dot_general(ids, hit, (((1,), (1,)), ((), ())), preferred_element_type=F32)
    return found[0:1].astype(jnp.int32)


def pre_kernel(position_ref, rate_ref, field_ref, out_ref):
    index = jnp.broadcast_to(slot_row(position_ref[...]), (NODES, LANES))
    rate = gather_lanes(jnp.broadcast_to(rate_ref[...], (8, LANES)), index[:8])
    for s in range(SOURCES):
        out_ref[s, 0:NODES] = gather_lanes(field_ref[pl.ds(s, NODES, stride=SOURCES), :], index)
        out_ref[s, NODES:CHUNK] = rate


def post_kernel(position_ref, field_ref, out_ref):
    index = jnp.broadcast_to(position_ref[...], (NODES, LANES))
    for s in range(SOURCES):
        out_ref[pl.ds(s, NODES, stride=SOURCES), :] = gather_lanes(field_ref[s], index)


def fill_block(core, mixed_ref, swapped_ref, u_ref, rate_ref, slices=range(4)):
    for n, which in enumerate(slices):
        for k in range(BLOCK):
            chunk = which * 4 + k // 2
            u_ref[n, k + 1] = jnp.where(core == k % 2, mixed_ref[chunk, 0:NODES], swapped_ref[chunk, 0:NODES])
    for k in range(BLOCK):
        rate_ref[k + 1] = jnp.where(
            core == k % 2, mixed_ref[k // 2, NODES:CHUNK], swapped_ref[k // 2, NODES:CHUNK]
        )


def local_sweep(counts, ends, first, flag, u_ref, p_refs, c_ref, e_refs, rate_ref, weights, lanes, added, has_first=None):
    for power in range(4):
        source = u_ref if power == 0 else p_refs[power - 1]
        for n, powers in enumerate(counts):
            if power >= len(powers):
                continue
            start = first(powers[power])

            def load(k, source=source, start=start, n=n):
                return source[n, start - 1 + k]

            def rates(k, start=start):
                return rate_ref[start + k]

            def store(k, v, y, n=n, power=power, start=start):
                p = y - v
                if power < 3:
                    p_refs[power][n, start + k] = p
                else:
                    c_ref[n, start + k] = correction(
                        p_refs[1][n, start + k], v, p,
                        flag * (u_ref[n, start + k] + STEP * p_refs[0][n, start + k]) if n == 0 else None,
                    )

            sweep(powers[power], load, rates, weights, lanes, store)
    if has_first is not None:
        for k in range(BLOCK + 2):
            e_refs[3][k] = jnp.where(has_first, c_ref[0, k], 0.0)
    for n, count in enumerate(ends):
        source = e_refs[n - 1] if n else c_ref.at[0] if has_first is None else e_refs[3]
        start = first(count)

        def load(k, source=source, start=start):
            return source[start - 1 + k]

        def rates(k, start=start):
            return rate_ref[start + k]

        def store(k, v, y, n=n, start=start):
            e_refs[n][start + k] = (1.0 - STEP) * v + STEP * y + added(n + 1, start + k)

        sweep(count, load, rates, weights, lanes, store)


def clear_sides(u_ref, p_refs, c_ref, e_refs):
    for k in (0, BLOCK + 1):
        for ref in (u_ref, *p_refs, c_ref):
            for n in range(ref.shape[0]):
                ref[n, k] = jnp.zeros(LAYER, F32)
        for ref in e_refs:
            ref[k] = jnp.zeros(LAYER, F32)


def correction(second, third, fourth, more=None):
    total = (STEP**2 / 2) * second + (STEP**3 / 6) * third + (STEP**4 / 24) * fourth
    return total if more is None else total + more


def early_flag(flag_ref):
    return jnp.where(flag_ref[0] == 0, 1.0, 0.0).astype(F32)


def edge_kernel(flag_ref, w_ref, mixed_ref, swapped_ref, out_ref, u_ref, rate_ref, c_ref, *work):
    core = flag_ref[1]
    p_refs, e_refs = work[:3], work[3:]
    weights, lanes = stacked_weights(w_ref), neighbour_lanes()
    fill_block(core, mixed_ref, swapped_ref, u_ref, rate_ref)
    clear_sides(u_ref, p_refs, c_ref, e_refs)
    local_sweep(
        ((6, 6, 4, 4), (6, 4, 4, 2), (4, 4, 2, 2), (4, 2, 2)),
        (2, 2),
        lambda count: jnp.where(core == 0, 1, BLOCK + 1 - count),
        early_flag(flag_ref), u_ref, p_refs, c_ref, e_refs, rate_ref, weights, lanes,
        lambda n, layer: c_ref[n, layer],
    )
    edge = jnp.where(core == 0, 1, BLOCK)
    for t in range(TRACES):
        n, power = t // 4, t % 4
        if t < 16:
            layer = u_ref[n, edge] if power == 0 else p_refs[power - 1][n, edge]
        else:
            layer = c_ref[0, edge] if t == 16 else e_refs[t - 17][edge]
        out_ref[t * FACE : (t + 1) * FACE] = jnp.where(core == 0, layer[0:16], layer[48:64])
    out_ref[TRACES * FACE :] = jnp.concatenate([rate_ref[k + 1, 0:1] for k in range(BLOCK)], axis=0)


def block_kernel(flag_ref, w_ref, mixed_ref, swapped_ref, out_ref, u_ref, rate_ref, c_ref, *work):
    core = flag_ref[1]
    p_refs, e_refs = work[:3], work[3:]
    weights, lanes = stacked_weights(w_ref), neighbour_lanes()
    fill_block(core, mixed_ref, swapped_ref, u_ref, rate_ref, (core, 3 - core))
    clear_sides(u_ref, p_refs, c_ref, e_refs)

    def added(n, layer):
        return jnp.where(core == (0 if n == 3 else 1), c_ref[1 if n > 1 else 0, layer], 0.0)

    local_sweep(
        ((BLOCK,) * 4,) * 2, (BLOCK,) * 3, lambda count: 1,
        early_flag(flag_ref) * jnp.where(core == 0, 1.0, 0.0), u_ref, p_refs, c_ref, e_refs, rate_ref,
        weights, lanes, added, core == 0,
    )
    for k in range(BLOCK):
        out_ref[0, k] = e_refs[3][k + 1]
        for n in range(3):
            out_ref[n + 1, k] = e_refs[n][k + 1]


def respond(flag_ref, w_ref, sent_ref, got_ref, local_ref, base_ref, rest_ref, rate_ref, c_ref, work):
    core = flag_ref[1]
    p_refs, e_refs = work[:3], work[3:]
    weights, lanes = stacked_weights(w_ref), neighbour_lanes()
    flag = early_flag(flag_ref)
    for ref, reach in ((c_ref.at[0], 4), (e_refs[0], 5), (e_refs[1], 6), (e_refs[2], 7)):
        for k in range(BLOCK - reach):
            ref[k] = jnp.zeros(LAYER, F32)
            ref[2 * BLOCK - 1 - k] = jnp.zeros(LAYER, F32)
    for k in range(BLOCK):
        row = TRACES * FACE + k
        mine = jnp.broadcast_to(sent_ref[row : row + 1], (8, LANES))
        theirs = jnp.broadcast_to(got_ref[row : row + 1], (8, LANES))
        rate_ref[k] = jnp.where(core == 0, theirs, mine)
        rate_ref[BLOCK + k] = jnp.where(core == 0, mine, theirs)

    def step(reach, source, trace, store):
        start = BLOCK - reach
        mine, theirs = (r[trace * FACE : (trace + 1) * FACE] for r in (sent_ref, got_ref))

        def inject(k):
            if start + k == BLOCK - 1:
                return None, jnp.where(core == 0, mine, theirs)
            if start + k == BLOCK:
                return jnp.where(core == 0, theirs, mine), None
            return None, None

        def load(k):
            layer = start - 1 + k
            if not BLOCK - reach < layer < BLOCK + reach - 1:
                return jnp.zeros(LAYER, F32)
            return source(layer)

        sweep(
            2 * reach, load, lambda k: rate_ref[start + k], weights, lanes,
            lambda k, v, y: store(start + k, v, y), inject,
        )

    for power in range(4):
        for n in range(4):

            def source(layer, n=n, power=power):
                return p_refs[power - 1][n, layer]

            def store(layer, v, y, n=n, power=power):
                p = y - v
                if power < 3:
                    p_refs[power][n, layer] = p
                    return
                second = p_refs[1][n, layer] if BLOCK - 2 <= layer < BLOCK + 2 else 0.0
                more = None
                if n == 0 and BLOCK - 1 <= layer < BLOCK + 1:
                    more = flag * (STEP * p_refs[0][n, layer])
                c_ref[n, layer] = correction(second, v, p, more)

            step(power + 1, source, n * 4 + power, store)
    for n in range(3):

        def source(layer, n=n):
            return c_ref[0, layer] if n == 0 else e_refs[n - 1][layer]

        def store(layer, v, y, n=n):
            value = (1.0 - STEP) * v + STEP * y
            e_refs[n][layer] = value + c_ref[n + 1, layer] if BLOCK - 4 <= layer < BLOCK + 4 else value

        step(5 + n, source, 16 + n, store)

    side = jnp.where(core == 0, BLOCK, 0)
    for k in range(BLOCK):
        base_ref[0, k] = local_ref[0, k] + c_ref[0, side + k]
        for n in range(3):
            base_ref[n + 1, k] = local_ref[n + 1, k] + e_refs[n][side + k]
    for n in range(4):
        for x in range(4):
            rest_ref[n * 4 + x] = base_ref[n, 2 * x + 1 - core]


def early_kernel(flag_ref, w_ref, sent_ref, got_ref, local_ref, base_ref, last_ref, rest_ref, rate_ref, c_ref, *work):
    @pl.when(flag_ref[0] == 0)
    def _():
        respond(flag_ref, w_ref, sent_ref, got_ref, local_ref, base_ref, rest_ref, rate_ref, c_ref, work)
        for k in range(BLOCK):
            last_ref[k] = base_ref[3, k]

    last_ref[BLOCK, 0:BLOCK] = got_ref[TRACES * FACE :]


def join_kernel(flag_ref, base_ref, last_ref, own_ref, halo_ref):
    core = flag_ref[1]
    for k in range(4):
        layer = 4 * core + k
        own_ref[k] = base_ref[3, layer] + last_ref[layer]
        layer = 4 * (1 - core) + k
        halo_ref[k] = base_ref[3, layer] + last_ref[layer]


def late_kernel(
    flag_ref, w_ref, sent_ref, got_ref, local_ref, rest_in_ref, base_ref, rest_ref, rate_ref, c_ref, *work
):
    @pl.when(flag_ref[0] == 1)
    def _():
        respond(flag_ref, w_ref, sent_ref, got_ref, local_ref, base_ref, rest_ref, rate_ref, c_ref, work)

    @pl.when(flag_ref[0] == 0)
    def _():
        for k in range(16):
            rest_ref[k] = rest_in_ref[k]


def finish_kernel(
    flag_ref, w_ref, sent_ref, got_ref, base_ref, last_ref, late_base_ref, rest_ref,
    halo_ref, own_ref, halo_back_ref, own_back_ref, out_ref, rate_ref, start_ref, e_ref,
):
    core, late = flag_ref[1], flag_ref[0] == 1
    weights, lanes = stacked_weights(w_ref), neighbour_lanes()
    for k in range(4):
        start_ref[k] = jnp.where(core == 0, halo_ref[k], halo_back_ref[k])
        start_ref[4 + k] = jnp.where(core == 0, own_ref[k], own_back_ref[k])
        start_ref[8 + k] = jnp.where(core == 0, own_back_ref[k], own_ref[k])
        start_ref[12 + k] = jnp.where(core == 0, halo_back_ref[k], halo_ref[k])

    def row(ref, first, k):
        return jnp.broadcast_to(ref[first + k : first + k + 1], (8, LANES))

    for k in range(4):
        near, far = row(got_ref, TRACES * FACE, 4 + k), row(last_ref.at[BLOCK], 0, 4 + k)
        rate_ref[k] = jnp.where(core == 0, near, far)
        near, far = row(got_ref, TRACES * FACE, k), row(last_ref.at[BLOCK], 0, k)
        rate_ref[4 + BLOCK + k] = jnp.where(core == 0, far, near)
    for k in range(BLOCK):
        rate_ref[4 + k] = row(sent_ref, TRACES * FACE, k)
    for n in range(4):
        first = 1 + n
        source = start_ref if n == 0 else e_ref.at[n - 1]

        def store(k, v, y, n=n, first=first):
            e_ref[n, first + k] = (1.0 - STEP) * v + STEP * y

        sweep(
            2 * BLOCK - 2 * first,
            lambda k, source=source, first=first: source[first - 1 + k],
            lambda k, first=first: rate_ref[first + k],
            weights, lanes, store,
        )
    for n in range(4):
        for x in range(4):
            layer = 2 * x + core
            other = rest_ref[n * 4 + x]
            base = jnp.where(late, late_base_ref[n, layer], base_ref[n, layer])
            out_ref[n * 4 + x] = base + other + jnp.where(late, e_ref[n, 4 + layer], 0.0)


def call(kernel, outs, scratch, n_in, flags=True):
    whole = pl.BlockSpec(memory_space=pltpu.VMEM)
    first = [pl.BlockSpec(memory_space=pltpu.SMEM)] if flags else []
    return pl.pallas_call(
        kernel,
        out_shape=tuple(jax.ShapeDtypeStruct(s, F32) for s in outs),
        in_specs=first + [whole] * (n_in - len(first)),
        out_specs=tuple(whole for _ in outs),
        scratch_shapes=[pltpu.VMEM(s, F32) for s in scratch],
        compiler_params=pltpu.CompilerParams(vmem_limit_bytes=VMEM),
    )


LAYER = (NODES, LANES)
RATES = (8, LANES)


def shards(slice_start, volume, lift_matrix, element_rate, position, neighbours):
    del neighbours
    zh, core = lax.axis_index("zh"), lax.axis_index("c")
    flags = jnp.stack([zh, core]).astype(jnp.int32)
    weights = jnp.dot(
        jnp.concatenate([volume, lift_matrix], axis=1), jnp.asarray(selection()), precision=lax.Precision.HIGHEST
    )
    row = position.reshape(1, LANES)
    (natural,) = call(pre_kernel, ((SOURCES, CHUNK, LANES),), (), 3, False)(
        row, element_rate.reshape(1, LANES), slice_start.reshape(NODES * SOURCES, LANES)
    )
    swap = [(0, 1), (1, 0)]
    mixed = lax.all_to_all(natural, ("y", "x"), 0, 0, tiled=True)
    swapped = lax.ppermute(mixed, "c", swap)

    def block_scratch(slices, corrections, ends):
        inner = BLOCK + 2
        return (
            (slices, inner) + LAYER, (inner,) + RATES, (corrections, inner) + LAYER,
            *[(slices, inner) + LAYER] * 3, *[(inner,) + LAYER] * ends,
        )

    (sent,) = call(edge_kernel, ((TRACES * FACE + 8, LANES),), block_scratch(4, 3, 2), 4)(flags, weights, mixed, swapped)
    meet = [(z * 2 + c, (z + (-1, 1)[c]) % 4 * 2 + 1 - c) for z in range(4) for c in range(2)]
    got = lax.ppermute(sent, ("zl", "c"), meet)
    (local,) = call(block_kernel, ((4, BLOCK) + LAYER,), block_scratch(2, 2, 4), 4)(flags, weights, mixed, swapped)
    both = 2 * BLOCK
    scratch = ((both,) + RATES, *[(4, both) + LAYER] * 4, *[(both,) + LAYER] * 3)
    base, last, rest = call(
        early_kernel, ((4, BLOCK) + LAYER, (BLOCK + 1,) + LAYER, (16,) + LAYER), scratch, 5
    )(flags, weights, sent, got, local)
    last = lax.ppermute(last, "c", swap)

    halves = call(join_kernel, ((4,) + LAYER,) * 2, (), 3)(flags, base, last)
    own_half, halo_half, rest = lax.optimization_barrier((*halves, rest))
    straight = [(z * 2 + c, (4 + z) * 2 + c) for z in range(4) for c in range(2)]
    beside = [(z * 2 + c, (4 + (z + (1, -1)[c]) % 4) * 2 + c) for z in range(4) for c in range(2)]
    axes = ("zh", "zl", "c")
    halo = lax.ppermute(halo_half, axes, beside)
    own = lax.ppermute(own_half, axes, straight)
    late_base, rest = call(late_kernel, ((4, BLOCK) + LAYER, (16,) + LAYER), scratch, 6)(
        flags, weights, sent, got, local, rest
    )
    halo, own, rest = lax.optimization_barrier((halo, own, rest))
    rest = lax.ppermute(rest, "c", swap)
    (out,) = call(
        finish_kernel,
        ((SOURCES,) + LAYER,),
        ((2 * BLOCK,) + RATES, (2 * BLOCK,) + LAYER, (4, 2 * BLOCK) + LAYER),
        12,
    )(
        flags, weights, sent, got, base, last, late_base, rest,
        halo, own, lax.ppermute(halo, "c", swap), lax.ppermute(own, "c", swap),
    )
    home = lax.all_to_all(out, ("y", "x"), 0, 0, tiled=True)
    (final,) = call(post_kernel, ((NODES * SOURCES, LANES),), (), 2, False)(row, home)
    return final.reshape(slice_start.shape)


def solution(mesh):
    fine_mesh = Mesh(mesh.devices.reshape(2, 4, 4, 4, 2), ("zh", "y", "zl", "x", "c"))
    tm, space = ("zh", "y"), ("zl", "x", "c")
    placed = (P(tm, None, None, space), P(), P(), P(space), P(space), P(None, space))
    return jax.shard_map(
        shards, mesh=fine_mesh, in_specs=placed, out_specs=P(tm, None, None, space), check_vma=False
    )
```

```python
import functools

import jax
import jax.numpy as jnp
import numpy as np
from jax import lax
from jax.experimental import pallas as pl
from jax.experimental.pallas import tpu as pltpu
from jax.sharding import Mesh, PartitionSpec as P

STEP = 0.25
NODES = 64
LANES = 128
SOURCES = 16
COLS = 16
BLOCK = 8
CHUNK = 72
TRACES = 19
FACE = 16
RANK = 192
VMEM = 40 * 1024 * 1024
F32 = jnp.float32


def selection():
    table = np.zeros((160, RANK), np.float32)
    for a in range(4):
        for b in range(4):
            for c in range(4):
                node = a * 16 + b * 4 + c
                table[node, node] += 1.0
                faces = ((a, 0, b * 4 + c), (b, 2, a * 4 + c), (c, 4, a * 4 + b))
                for place, low, rank in faces:
                    if place == 0:
                        table[64 + low * 16 + rank, node] -= 1.0
                    if place == 3:
                        table[64 + (low + 1) * 16 + rank, node] -= 1.0
                if c == 0:
                    table[64 + 5 * 16 + a * 4 + b, 128 + node] = 1.0
                if c == 3:
                    table[64 + 4 * 16 + a * 4 + b, 128 + node] = 1.0
    for k in range(16):
        table[64 + k, 64 + k] = 1.0
        table[64 + 16 + k, 80 + k] = 1.0
    for a in range(4):
        for c in range(4):
            table[64 + 3 * 16 + a * 4 + c, 96 + a * 8 + c] = 1.0
            table[64 + 2 * 16 + a * 4 + c, 96 + a * 8 + 4 + c] = 1.0
    return table


def gather_lanes(x, index):
    return jnp.take_along_axis(x, index, axis=1, mode="promise_in_bounds")


def neighbour_lanes():
    lane = lax.broadcasted_iota(jnp.int32, (8, LANES), 1)
    row = lax.broadcasted_iota(jnp.int32, (8, LANES), 0)
    y_index = jnp.where(row < 4, lane + COLS, lane + (LANES - COLS)) & (LANES - 1)
    col = lane & (COLS - 1)
    z_step = jnp.where((row & 3) == 0, 1, COLS - 1)
    z_index = (lane - col) + ((col + z_step) & (COLS - 1))
    return y_index, z_index, row < 4


def operand(before, here, after, lanes):
    y_index, z_index, low = lanes
    ys = [
        gather_lanes(jnp.where(low, here[16 * a : 16 * a + 8], here[16 * a + 8 : 16 * a + 16]), y_index)
        for a in range(4)
    ]
    zs = [gather_lanes(here[8 * k : 8 * k + 8], z_index) for k in range(8)]
    return jnp.concatenate([here, before, after] + ys + zs, axis=0)


def split(x):
    high = x.astype(jnp.bfloat16)
    low = (x - high.astype(F32)).astype(jnp.bfloat16)
    return high, low


def product(weights, x):
    high, low = split(x)
    first = jnp.dot(weights, high, preferred_element_type=F32)
    second = jnp.dot(weights[:NODES], low, preferred_element_type=F32)
    return first[:NODES] + first[NODES:] + second


def stacked_weights(w_ref):
    high, low = split(w_ref[...])
    return jnp.concatenate([high, low], axis=0)


def sweep(count, load, rates, weights, lanes, store, inject=None):
    for k in range(0, count, 2):
        v = [load(k + i) for i in range(4)]
        x = []
        for i in range(2):
            before, after = v[i][48:64], v[i + 2][0:16]
            extra = inject(k + i) if inject is not None else (None, None)
            before = before if extra[0] is None else before + extra[0]
            after = after if extra[1] is None else after + extra[1]
            x.append(operand(before, v[i + 1], after, lanes))
        y = product(weights, jnp.concatenate(x, axis=1))
        for i in range(2):
            rate = jnp.concatenate([rates(k + i)] * (NODES // 8), axis=0)
            store(k + i, v[i + 1], rate * y[:, i * LANES : (i + 1) * LANES])


def slot_row(position):
    where = lax.broadcasted_iota(jnp.int32, (LANES, LANES), 0)
    hit = jnp.where(position == where, 1.0, 0.0).astype(jnp.bfloat16)
    ids = lax.broadcasted_iota(jnp.int32, (16, LANES), 1).astype(F32).astype(jnp.bfloat16)
    found = lax.dot_general(ids, hit, (((1,), (1,)), ((), ())), preferred_element_type=F32)
    return found[0:1].astype(jnp.int32)


PARTS = 4
PART_NODES = NODES // PARTS
PART_ROWS = PART_NODES * SOURCES


def pre_kernel(position_ref, rate_ref, field_ref, out_ref):
    index = jnp.broadcast_to(slot_row(position_ref[...]), (NODES, LANES))
    rate = gather_lanes(jnp.broadcast_to(rate_ref[...], (8, LANES)), index[:8])
    for s in range(SOURCES):
        out_ref[s, 0:NODES] = gather_lanes(field_ref[pl.ds(s, NODES, stride=SOURCES), :], index)
        out_ref[s, NODES:CHUNK] = rate


def post_kernel(position_ref, field_ref, out_hbm, out_ref, sems):
    index = jnp.broadcast_to(position_ref[...], (PART_NODES, LANES))
    copies = []
    for part in range(PARTS):
        for s in range(SOURCES):
            piece = gather_lanes(field_ref[s, part * PART_NODES : (part + 1) * PART_NODES], index)
            out_ref[pl.ds(part * PART_ROWS + s, PART_NODES, stride=SOURCES), :] = piece
        rows = pl.ds(part * PART_ROWS, PART_ROWS)
        copies.append(pltpu.make_async_copy(out_ref.at[rows], out_hbm.at[rows], sems.at[part]))
        copies[-1].start()
    for copy in copies:
        copy.wait()


def fill_block(core, mixed_ref, swapped_ref, u_ref, rate_ref, slices=range(4)):
    for n, which in enumerate(slices):
        for k in range(BLOCK):
            chunk = which * 4 + k // 2
            u_ref[n, k + 1] = jnp.where(core == k % 2, mixed_ref[chunk, 0:NODES], swapped_ref[chunk, 0:NODES])
    for k in range(BLOCK):
        rate_ref[k + 1] = jnp.where(
            core == k % 2, mixed_ref[k // 2, NODES:CHUNK], swapped_ref[k // 2, NODES:CHUNK]
        )


def local_sweep(counts, ends, first, flag, u_ref, p_refs, c_ref, e_refs, rate_ref, weights, lanes, added, has_first=None):
    for power in range(4):
        source = u_ref if power == 0 else p_refs[power - 1]
        for n, powers in enumerate(counts):
            if power >= len(powers):
                continue
            start = first(powers[power])

            def load(k, source=source, start=start, n=n):
                return source[n, start - 1 + k]

            def rates(k, start=start):
                return rate_ref[start + k]

            def store(k, v, y, n=n, power=power, start=start):
                p = y - v
                if power < 3:
                    p_refs[power][n, start + k] = p
                else:
                    c_ref[n, start + k] = correction(
                        p_refs[1][n, start + k], v, p,
                        flag * (u_ref[n, start + k] + STEP * p_refs[0][n, start + k]) if n == 0 else None,
                    )

            sweep(powers[power], load, rates, weights, lanes, store)
    if has_first is not None:
        for k in range(BLOCK + 2):
            e_refs[3][k] = jnp.where(has_first, c_ref[0, k], 0.0)
    for n, count in enumerate(ends):
        source = e_refs[n - 1] if n else c_ref.at[0] if has_first is None else e_refs[3]
        start = first(count)

        def load(k, source=source, start=start):
            return source[start - 1 + k]

        def rates(k, start=start):
            return rate_ref[start + k]

        def store(k, v, y, n=n, start=start):
            e_refs[n][start + k] = (1.0 - STEP) * v + STEP * y + added(n + 1, start + k)

        sweep(count, load, rates, weights, lanes, store)


def clear_sides(u_ref, p_refs, c_ref, e_refs):
    for k in (0, BLOCK + 1):
        for ref in (u_ref, *p_refs, c_ref):
            for n in range(ref.shape[0]):
                ref[n, k] = jnp.zeros(LAYER, F32)
        for ref in e_refs:
            ref[k] = jnp.zeros(LAYER, F32)


def correction(second, third, fourth, more=None):
    total = (STEP**2 / 2) * second + (STEP**3 / 6) * third + (STEP**4 / 24) * fourth
    return total if more is None else total + more


def early_flag(flag_ref):
    return jnp.where(flag_ref[0] == 0, 1.0, 0.0).astype(F32)


def edge_kernel(flag_ref, w_ref, mixed_ref, swapped_ref, out_ref, u_ref, rate_ref, c_ref, *work):
    core = flag_ref[1]
    p_refs, e_refs = work[:3], work[3:]
    weights, lanes = stacked_weights(w_ref), neighbour_lanes()
    fill_block(core, mixed_ref, swapped_ref, u_ref, rate_ref)
    clear_sides(u_ref, p_refs, c_ref, e_refs)
    local_sweep(
        ((6, 6, 4, 4), (6, 4, 4, 2), (4, 4, 2, 2), (4, 2, 2)),
        (2, 2),
        lambda count: jnp.where(core == 0, 1, BLOCK + 1 - count),
        early_flag(flag_ref), u_ref, p_refs, c_ref, e_refs, rate_ref, weights, lanes,
        lambda n, layer: c_ref[n, layer],
    )
    edge = jnp.where(core == 0, 1, BLOCK)
    for t in range(TRACES):
        n, power = t // 4, t % 4
        if t < 16:
            layer = u_ref[n, edge] if power == 0 else p_refs[power - 1][n, edge]
        else:
            layer = c_ref[0, edge] if t == 16 else e_refs[t - 17][edge]
        out_ref[t * FACE : (t + 1) * FACE] = jnp.where(core == 0, layer[0:16], layer[48:64])
    out_ref[TRACES * FACE :] = jnp.concatenate([rate_ref[k + 1, 0:1] for k in range(BLOCK)], axis=0)


def own_ends(flag_ref, w_ref, mixed_ref, swapped_ref, out_ref, u_ref, rate_ref, c_ref, *work):
    core = flag_ref[1]
    p_refs, e_refs = work[:3], work[3:]
    weights, lanes = stacked_weights(w_ref), neighbour_lanes()
    fill_block(core, mixed_ref, swapped_ref, u_ref, rate_ref, (core, 3 - core))
    clear_sides(u_ref, p_refs, c_ref, e_refs)

    def added(n, layer):
        return jnp.where(core == (0 if n == 3 else 1), c_ref[1 if n > 1 else 0, layer], 0.0)

    local_sweep(
        ((BLOCK,) * 4,) * 2, (BLOCK,) * 3, lambda count: 1,
        early_flag(flag_ref) * jnp.where(core == 0, 1.0, 0.0), u_ref, p_refs, c_ref, e_refs, rate_ref,
        weights, lanes, added, core == 0,
    )
    for k in range(BLOCK):
        out_ref[0, k] = e_refs[3][k + 1]
        for n in range(3):
            out_ref[n + 1, k] = e_refs[n][k + 1]


def block_kernel(flag_ref, w_ref, mixed_ref, swapped_ref, out_ref, *work):
    @pl.when(flag_ref[0] == 0)
    def _():
        own_ends(flag_ref, w_ref, mixed_ref, swapped_ref, out_ref, *work)


def respond(flag_ref, w_ref, sent_ref, got_ref, local_ref, base_ref, rest_ref, rate_ref, c_ref, work):
    core = flag_ref[1]
    p_refs, e_refs = work[:3], work[3:]
    weights, lanes = stacked_weights(w_ref), neighbour_lanes()
    flag = early_flag(flag_ref)
    for ref, reach in ((c_ref.at[0], 4), (e_refs[0], 5), (e_refs[1], 6), (e_refs[2], 7)):
        for k in range(BLOCK - reach):
            ref[k] = jnp.zeros(LAYER, F32)
            ref[2 * BLOCK - 1 - k] = jnp.zeros(LAYER, F32)
    for k in range(BLOCK):
        row = TRACES * FACE + k
        mine = jnp.broadcast_to(sent_ref[row : row + 1], (8, LANES))
        theirs = jnp.broadcast_to(got_ref[row : row + 1], (8, LANES))
        rate_ref[k] = jnp.where(core == 0, theirs, mine)
        rate_ref[BLOCK + k] = jnp.where(core == 0, mine, theirs)

    def step(reach, source, trace, store):
        start = BLOCK - reach
        mine, theirs = (r[trace * FACE : (trace + 1) * FACE] for r in (sent_ref, got_ref))

        def inject(k):
            if start + k == BLOCK - 1:
                return None, jnp.where(core == 0, mine, theirs)
            if start + k == BLOCK:
                return jnp.where(core == 0, theirs, mine), None
            return None, None

        def load(k):
            layer = start - 1 + k
            if not BLOCK - reach < layer < BLOCK + reach - 1:
                return jnp.zeros(LAYER, F32)
            return source(layer)

        sweep(
            2 * reach, load, lambda k: rate_ref[start + k], weights, lanes,
            lambda k, v, y: store(start + k, v, y), inject,
        )

    for power in range(4):
        for n in range(4):

            def source(layer, n=n, power=power):
                return p_refs[power - 1][n, layer]

            def store(layer, v, y, n=n, power=power):
                p = y - v
                if power < 3:
                    p_refs[power][n, layer] = p
                    return
                second = p_refs[1][n, layer] if BLOCK - 2 <= layer < BLOCK + 2 else 0.0
                more = None
                if n == 0 and BLOCK - 1 <= layer < BLOCK + 1:
                    more = flag * (STEP * p_refs[0][n, layer])
                c_ref[n, layer] = correction(second, v, p, more)

            step(power + 1, source, n * 4 + power, store)
    for n in range(3):

        def source(layer, n=n):
            return c_ref[0, layer] if n == 0 else e_refs[n - 1][layer]

        def store(layer, v, y, n=n):
            value = (1.0 - STEP) * v + STEP * y
            e_refs[n][layer] = value + c_ref[n + 1, layer] if BLOCK - 4 <= layer < BLOCK + 4 else value

        step(5 + n, source, 16 + n, store)

    side = jnp.where(core == 0, BLOCK, 0)
    for k in range(BLOCK):
        base_ref[0, k] = local_ref[0, k] + c_ref[0, side + k]
        for n in range(3):
            base_ref[n + 1, k] = local_ref[n + 1, k] + e_refs[n][side + k]
    for n in range(4):
        for x in range(4):
            rest_ref[n * 4 + x] = base_ref[n, 2 * x + 1 - core]


def early_kernel(flag_ref, w_ref, sent_ref, got_ref, local_ref, base_ref, last_ref, rest_ref, rate_ref, c_ref, *work):
    @pl.when(flag_ref[0] == 0)
    def _():
        respond(flag_ref, w_ref, sent_ref, got_ref, local_ref, base_ref, rest_ref, rate_ref, c_ref, work)
        for k in range(BLOCK):
            last_ref[k] = base_ref[3, k]


def join_kernel(flag_ref, w_ref, sent_ref, base_ref, last_ref, own_ref, out_ref, rate_ref, *e_refs):
    core = flag_ref[1]

    @pl.when(flag_ref[0] == 0)
    def _():
        weights, lanes = stacked_weights(w_ref), neighbour_lanes()
        for k in (0, BLOCK + 1):
            for ref in e_refs:
                ref[k] = jnp.zeros(LAYER, F32)
        for k in range(BLOCK):
            e_refs[0][k + 1] = base_ref[3, k] + last_ref[k]
            rate_ref[k + 1] = jnp.broadcast_to(sent_ref[TRACES * FACE + k : TRACES * FACE + k + 1], (8, LANES))
        for k in range(4):
            own_ref[k] = e_refs[0][1 + 4 * core + k]
        for n, count in enumerate((4, 2, 2)):
            start = jnp.where(core == 0, BLOCK + 1 - count, 1)

            def store(k, v, y, n=n, start=start):
                e_refs[n + 1][start + k] = (1.0 - STEP) * v + STEP * y

            sweep(
                count,
                lambda k, n=n, start=start: e_refs[n][start - 1 + k],
                lambda k, start=start: rate_ref[start + k],
                weights, lanes, store,
            )
        edge = jnp.where(core == 0, BLOCK, 1)
        for n in range(4):
            layer = e_refs[n][edge]
            out_ref[n * FACE : (n + 1) * FACE] = jnp.where(core == 0, layer[48:64], layer[0:16])


def late_kernel(
    flag_ref, w_ref, mixed_ref, swapped_ref, sent_ref, got_ref, rest_in_ref, base_ref, rest_ref, local_ref, *work
):
    @pl.when(flag_ref[0] == 1)
    def _():
        own_ends(flag_ref, w_ref, mixed_ref, swapped_ref, local_ref, *work[:10])
        respond(flag_ref, w_ref, sent_ref, got_ref, local_ref, base_ref, rest_ref, work[10], work[11], work[12:])

    @pl.when(flag_ref[0] == 0)
    def _():
        for k in range(16):
            rest_ref[k] = rest_in_ref[k]

    rest_ref[16, 0:BLOCK] = got_ref[TRACES * FACE :]


def finish_kernel(
    flag_ref, w_ref, sent_ref, got_ref, base_ref, late_base_ref, rest_ref,
    halo_ref, own_ref, halo_back_ref, own_back_ref, out_ref, rate_ref, start_ref, *e_refs,
):
    core = flag_ref[1]

    def row(ref, k):
        return jnp.broadcast_to(ref[k : k + 1], (8, LANES))

    @pl.when(flag_ref[0] == 1)
    def _():
        weights, lanes = stacked_weights(w_ref), neighbour_lanes()
        for k in range(4):
            start_ref[4 + k] = jnp.where(core == 0, own_ref[k], own_back_ref[k])
            start_ref[8 + k] = jnp.where(core == 0, own_back_ref[k], own_ref[k])
        for k in range(4):
            near, far = row(got_ref, TRACES * FACE + 4 + k), row(rest_ref.at[16], 4 + k)
            rate_ref[k] = jnp.where(core == 0, near, far)
            near, far = row(got_ref, TRACES * FACE + k), row(rest_ref.at[16], k)
            rate_ref[4 + BLOCK + k] = jnp.where(core == 0, far, near)
        for k in range(BLOCK):
            rate_ref[4 + k] = row(sent_ref, TRACES * FACE + k)
        for n in range(4):
            first = 1 + n
            source = start_ref if n == 0 else e_refs[n - 1]
            mine, theirs = (r[n * FACE : (n + 1) * FACE] for r in (halo_ref, halo_back_ref))
            sides = (jnp.where(core == 0, mine, theirs), jnp.where(core == 0, theirs, mine))

            def load(k, n=n, source=source, first=first):
                layer = first - 1 + k
                return source[layer] if 4 - n <= layer < 12 + n else jnp.zeros(LAYER, F32)

            def inject(k, first=first, sides=sides):
                return (sides[0] if first + k == 4 else None, sides[1] if first + k == 11 else None)

            def store(k, v, y, n=n, first=first):
                e_refs[n][first + k] = (1.0 - STEP) * v + STEP * y

            sweep(
                2 * BLOCK - 2 * first, load, lambda k, first=first: rate_ref[first + k],
                weights, lanes, store, inject,
            )
            for x in range(4):
                layer = 2 * x + core
                out_ref[n * 4 + x] = late_base_ref[n, layer] + rest_ref[n * 4 + x] + e_refs[n][4 + layer]

    @pl.when(flag_ref[0] == 0)
    def _():
        for n in range(4):
            for x in range(4):
                out_ref[n * 4 + x] = base_ref[n, 2 * x + core] + rest_ref[n * 4 + x]


def call(kernel, outs, scratch, n_in, flags=True):
    whole = pl.BlockSpec(memory_space=pltpu.VMEM)
    first = [pl.BlockSpec(memory_space=pltpu.SMEM)] if flags else []
    return pl.pallas_call(
        kernel,
        out_shape=tuple(jax.ShapeDtypeStruct(s, F32) for s in outs),
        in_specs=first + [whole] * (n_in - len(first)),
        out_specs=tuple(whole for _ in outs),
        scratch_shapes=[pltpu.VMEM(s, F32) for s in scratch],
        compiler_params=pltpu.CompilerParams(vmem_limit_bytes=VMEM),
    )


def leave(position, field):
    whole = pl.BlockSpec(memory_space=pltpu.VMEM)
    return pl.pallas_call(
        post_kernel,
        out_shape=jax.ShapeDtypeStruct((NODES * SOURCES, LANES), F32),
        in_specs=[whole] * 2,
        out_specs=pl.BlockSpec(memory_space=pltpu.HBM),
        scratch_shapes=[pltpu.VMEM((NODES * SOURCES, LANES), F32), pltpu.SemaphoreType.DMA((PARTS,))],
        compiler_params=pltpu.CompilerParams(vmem_limit_bytes=VMEM),
    )(position, field)


LAYER = (NODES, LANES)
RATES = (8, LANES)


def shards(slice_start, volume, lift_matrix, element_rate, position, neighbours):
    del neighbours
    zh, core = lax.axis_index("zh"), lax.axis_index("c")
    flags = jnp.stack([zh, core]).astype(jnp.int32)
    weights = jnp.dot(
        jnp.concatenate([volume, lift_matrix], axis=1), jnp.asarray(selection()), precision=lax.Precision.HIGHEST
    )
    row = position.reshape(1, LANES)
    (natural,) = call(pre_kernel, ((SOURCES, CHUNK, LANES),), (), 3, False)(
        row, element_rate.reshape(1, LANES), slice_start.reshape(NODES * SOURCES, LANES)
    )
    swap = [(0, 1), (1, 0)]
    mixed = lax.all_to_all(natural, ("y", "x"), 0, 0, tiled=True)
    swapped = lax.ppermute(mixed, "c", swap)

    def block_scratch(slices, corrections, ends):
        inner = BLOCK + 2
        return (
            (slices, inner) + LAYER, (inner,) + RATES, (corrections, inner) + LAYER,
            *[(slices, inner) + LAYER] * 3, *[(inner,) + LAYER] * ends,
        )

    (sent,) = call(edge_kernel, ((TRACES * FACE + 8, LANES),), block_scratch(4, 3, 2), 4)(flags, weights, mixed, swapped)
    axes = ("zh", "zl", "c")

    def meet(half):
        first = half * 4
        return [((first + z) * 2 + c, (first + (z + (-1, 1)[c]) % 4) * 2 + 1 - c) for z in range(4) for c in range(2)]

    got = lax.ppermute(sent, axes, meet(0))
    (local,) = call(block_kernel, ((4, BLOCK) + LAYER,), block_scratch(2, 2, 4), 4)(flags, weights, mixed, swapped)
    both = 2 * BLOCK
    scratch = ((both,) + RATES, *[(4, both) + LAYER] * 4, *[(both,) + LAYER] * 3)
    base, last, rest = call(
        early_kernel, ((4, BLOCK) + LAYER, (BLOCK,) + LAYER, (16,) + LAYER), scratch, 5
    )(flags, weights, sent, got, local)
    last = lax.ppermute(last, "c", swap)

    own_half, faces = call(
        join_kernel, ((4,) + LAYER, (4 * FACE, LANES)), ((BLOCK + 2,) + RATES, *[(BLOCK + 2,) + LAYER] * 4), 5
    )(flags, weights, sent, base, last)
    own_half, faces, rest, late_sent = lax.optimization_barrier((own_half, faces, rest, sent))
    straight = [(z * 2 + c, (4 + z) * 2 + c) for z in range(4) for c in range(2)]
    beside = [(z * 2 + c, (4 + (z + (1, -1)[c]) % 4) * 2 + c) for z in range(4) for c in range(2)]
    own = lax.ppermute(own_half, axes, straight)
    halo = lax.ppermute(faces, axes, beside)
    got = lax.ppermute(late_sent, axes, meet(1))
    late_base, rest = call(
        late_kernel,
        ((4, BLOCK) + LAYER, (17,) + LAYER),
        ((4, BLOCK) + LAYER, *block_scratch(2, 2, 4), *scratch),
        7,
    )(flags, weights, mixed, swapped, sent, got, rest)
    halo, own, rest = lax.optimization_barrier((halo, own, rest))
    rest = lax.ppermute(rest, "c", swap)
    (out,) = call(
        finish_kernel,
        ((SOURCES,) + LAYER,),
        ((both,) + RATES, (both,) + LAYER, *[(both,) + LAYER] * 4),
        11,
    )(
        flags, weights, sent, got, base, late_base, rest,
        halo, own, lax.ppermute(halo, "c", swap), lax.ppermute(own, "c", swap),
    )
    home = lax.all_to_all(out, ("y", "x"), 0, 0, tiled=True)
    return leave(row, home).reshape(slice_start.shape)


def solution(mesh):
    fine_mesh = Mesh(mesh.devices.reshape(2, 4, 4, 4, 2), ("zh", "y", "zl", "x", "c"))
    tm, space = ("zh", "y"), ("zl", "x", "c")
    placed = (P(tm, None, None, space), P(), P(), P(space), P(space), P(None, space))
    return jax.shard_map(
        shards, mesh=fine_mesh, in_specs=placed, out_specs=P(tm, None, None, space), check_vma=False
    )
```

```python
import functools

import jax
import jax.numpy as jnp
import numpy as np
from jax import lax
from jax.experimental import pallas as pl
from jax.experimental.pallas import tpu as pltpu
from jax.sharding import Mesh, PartitionSpec as P

STEP = 0.25
NODES = 64
LANES = 128
SOURCES = 16
COLS = 16
BLOCK = 8
CHUNK = 72
TRACES = 19
FACE = 16
RANK = 160
VMEM = 40 * 1024 * 1024
F32 = jnp.float32


def selection():
    table = np.zeros((160, RANK), np.float32)
    for a in range(4):
        for b in range(4):
            for c in range(4):
                node = a * 16 + b * 4 + c
                table[node, node] += 1.0
                faces = ((a, 0, b * 4 + c), (b, 2, a * 4 + c), (c, 4, a * 4 + b))
                for place, low, rank in faces:
                    if place == 0:
                        table[64 + low * 16 + rank, node] -= 1.0
                    if place == 3:
                        table[64 + (low + 1) * 16 + rank, node] -= 1.0
                place = 128 + a * 8 + (node % 8 + (2 if node % 16 >= 8 else 0)) % 8
                if c == 0:
                    table[64 + 5 * 16 + a * 4 + b, place] = 1.0
                if c == 3:
                    table[64 + 4 * 16 + a * 4 + b, place] = 1.0
    for k in range(16):
        table[64 + k, 64 + k] = 1.0
        table[64 + 16 + k, 80 + k] = 1.0
    for a in range(4):
        for c in range(4):
            table[64 + 3 * 16 + a * 4 + c, 96 + a * 8 + c] = 1.0
            table[64 + 2 * 16 + a * 4 + c, 96 + a * 8 + 4 + c] = 1.0
    return table


def gather_lanes(x, index):
    return jnp.take_along_axis(x, index, axis=1, mode="promise_in_bounds")


def neighbour_lanes():
    lane = lax.broadcasted_iota(jnp.int32, (8, LANES), 1)
    row = lax.broadcasted_iota(jnp.int32, (8, LANES), 0)
    y_index = jnp.where(row < 4, lane + COLS, lane + (LANES - COLS)) & (LANES - 1)
    col = lane & (COLS - 1)
    z_step = jnp.where((row & 1) == 0, 1, COLS - 1)
    z_index = (lane - col) + ((col + z_step) & (COLS - 1))
    return y_index, z_index, row < 4, ((row + 1) & 3) < 2


def operand(before, here, after, lanes):
    y_index, z_index, low, outer = lanes
    ys = [
        gather_lanes(jnp.where(low, here[16 * a : 16 * a + 8], here[16 * a + 8 : 16 * a + 16]), y_index)
        for a in range(4)
    ]
    zs = [
        gather_lanes(
            jnp.where(outer, here[16 * a : 16 * a + 8], pltpu.roll(here[16 * a + 8 : 16 * a + 16], 2, 0)), z_index
        )
        for a in range(4)
    ]
    return jnp.concatenate([here, before, after] + ys + zs, axis=0)


def split(x):
    high = x.astype(jnp.bfloat16)
    low = (x - high.astype(F32)).astype(jnp.bfloat16)
    return high, low


def product(weights, x):
    high, low = split(x)
    first = jnp.dot(weights, high, preferred_element_type=F32)
    second = jnp.dot(weights[:NODES], low, preferred_element_type=F32)
    return first[:NODES] + first[NODES:] + second


def stacked_weights(w_ref):
    high, low = split(w_ref[...])
    return jnp.concatenate([high, low], axis=0)


def sweep(count, load, rates, weights, lanes, store, inject=None):
    for k in range(0, count, 2):
        v = [load(k + i) for i in range(4)]
        x = []
        for i in range(2):
            before, after = v[i][48:64], v[i + 2][0:16]
            extra = inject(k + i) if inject is not None else (None, None)
            before = before if extra[0] is None else before + extra[0]
            after = after if extra[1] is None else after + extra[1]
            x.append(operand(before, v[i + 1], after, lanes))
        y = product(weights, jnp.concatenate(x, axis=1))
        for i in range(2):
            rate = jnp.concatenate([rates(k + i)] * (NODES // 8), axis=0)
            store(k + i, v[i + 1], rate * y[:, i * LANES : (i + 1) * LANES])


def slot_row(position):
    where = lax.broadcasted_iota(jnp.int32, (LANES, LANES), 0)
    hit = jnp.where(position == where, 1.0, 0.0).astype(jnp.bfloat16)
    ids = lax.broadcasted_iota(jnp.int32, (16, LANES), 1).astype(F32).astype(jnp.bfloat16)
    found = lax.dot_general(ids, hit, (((1,), (1,)), ((), ())), preferred_element_type=F32)
    return found[0:1].astype(jnp.int32)


PARTS = 4
PART_NODES = NODES // PARTS
PART_ROWS = PART_NODES * SOURCES


def pre_kernel(position_ref, rate_ref, field_ref, out_ref):
    index = jnp.broadcast_to(slot_row(position_ref[...]), (NODES, LANES))
    rate = gather_lanes(jnp.broadcast_to(rate_ref[...], (8, LANES)), index[:8])
    for s in range(SOURCES):
        out_ref[s, 0:NODES] = gather_lanes(field_ref[pl.ds(s, NODES, stride=SOURCES), :], index)
        out_ref[s, NODES:CHUNK] = rate


def post_kernel(position_ref, field_ref, out_hbm, out_ref, sems):
    index = jnp.broadcast_to(position_ref[...], (PART_NODES, LANES))
    copies = []
    for part in range(PARTS):
        for s in range(SOURCES):
            piece = gather_lanes(field_ref[s, part * PART_NODES : (part + 1) * PART_NODES], index)
            out_ref[pl.ds(part * PART_ROWS + s, PART_NODES, stride=SOURCES), :] = piece
        rows = pl.ds(part * PART_ROWS, PART_ROWS)
        copies.append(pltpu.make_async_copy(out_ref.at[rows], out_hbm.at[rows], sems.at[part]))
        copies[-1].start()
    for copy in copies:
        copy.wait()


def fill_block(core, mixed_ref, swapped_ref, u_ref, rate_ref, slices=range(4)):
    for n, which in enumerate(slices):
        for k in range(BLOCK):
            chunk = which * 4 + k // 2
            u_ref[n, k + 1] = jnp.where(core == k % 2, mixed_ref[chunk, 0:NODES], swapped_ref[chunk, 0:NODES])
    for k in range(BLOCK):
        rate_ref[k + 1] = jnp.where(
            core == k % 2, mixed_ref[k // 2, NODES:CHUNK], swapped_ref[k // 2, NODES:CHUNK]
        )


def local_sweep(counts, ends, first, flag, u_ref, p_refs, c_ref, e_refs, rate_ref, weights, lanes, added, has_first=None):
    for power in range(4):
        source = u_ref if power == 0 else p_refs[power - 1]
        for n, powers in enumerate(counts):
            if power >= len(powers):
                continue
            start = first(powers[power])

            def load(k, source=source, start=start, n=n):
                return source[n, start - 1 + k]

            def rates(k, start=start):
                return rate_ref[start + k]

            def store(k, v, y, n=n, power=power, start=start):
                p = y - v
                if power < 3:
                    p_refs[power][n, start + k] = p
                else:
                    c_ref[n, start + k] = correction(
                        p_refs[1][n, start + k], v, p,
                        flag * (u_ref[n, start + k] + STEP * p_refs[0][n, start + k]) if n == 0 else None,
                    )

            sweep(powers[power], load, rates, weights, lanes, store)
    if has_first is not None:
        for k in range(BLOCK + 2):
            e_refs[3][k] = jnp.where(has_first, c_ref[0, k], 0.0)
    for n, count in enumerate(ends):
        source = e_refs[n - 1] if n else c_ref.at[0] if has_first is None else e_refs[3]
        start = first(count)

        def load(k, source=source, start=start):
            return source[start - 1 + k]

        def rates(k, start=start):
            return rate_ref[start + k]

        def store(k, v, y, n=n, start=start):
            e_refs[n][start + k] = (1.0 - STEP) * v + STEP * y + added(n + 1, start + k)

        sweep(count, load, rates, weights, lanes, store)


def clear_sides(u_ref, p_refs, c_ref, e_refs):
    for k in (0, BLOCK + 1):
        for ref in (u_ref, *p_refs, c_ref):
            for n in range(ref.shape[0]):
                ref[n, k] = jnp.zeros(LAYER, F32)
        for ref in e_refs:
            ref[k] = jnp.zeros(LAYER, F32)


def correction(second, third, fourth, more=None):
    total = (STEP**2 / 2) * second + (STEP**3 / 6) * third + (STEP**4 / 24) * fourth
    return total if more is None else total + more


def early_flag(flag_ref):
    return jnp.where(flag_ref[0] == 0, 1.0, 0.0).astype(F32)


def edge_kernel(flag_ref, w_ref, mixed_ref, swapped_ref, out_ref, u_ref, rate_ref, c_ref, *work):
    core = flag_ref[1]
    p_refs, e_refs = work[:3], work[3:]
    weights, lanes = stacked_weights(w_ref), neighbour_lanes()
    fill_block(core, mixed_ref, swapped_ref, u_ref, rate_ref)
    clear_sides(u_ref, p_refs, c_ref, e_refs)
    local_sweep(
        ((6, 6, 4, 4), (6, 4, 4, 2), (4, 4, 2, 2), (4, 2, 2)),
        (2, 2),
        lambda count: jnp.where(core == 0, 1, BLOCK + 1 - count),
        early_flag(flag_ref), u_ref, p_refs, c_ref, e_refs, rate_ref, weights, lanes,
        lambda n, layer: c_ref[n, layer],
    )
    edge = jnp.where(core == 0, 1, BLOCK)
    for t in range(TRACES):
        n, power = t // 4, t % 4
        if t < 16:
            layer = u_ref[n, edge] if power == 0 else p_refs[power - 1][n, edge]
        else:
            layer = c_ref[0, edge] if t == 16 else e_refs[t - 17][edge]
        out_ref[t * FACE : (t + 1) * FACE] = jnp.where(core == 0, layer[0:16], layer[48:64])
    out_ref[TRACES * FACE :] = jnp.concatenate([rate_ref[k + 1, 0:1] for k in range(BLOCK)], axis=0)


def own_ends(flag_ref, w_ref, mixed_ref, swapped_ref, out_ref, u_ref, rate_ref, c_ref, *work):
    core = flag_ref[1]
    p_refs, e_refs = work[:3], work[3:]
    weights, lanes = stacked_weights(w_ref), neighbour_lanes()
    fill_block(core, mixed_ref, swapped_ref, u_ref, rate_ref, (core, 3 - core))
    clear_sides(u_ref, p_refs, c_ref, e_refs)

    def added(n, layer):
        return jnp.where(core == (0 if n == 3 else 1), c_ref[1 if n > 1 else 0, layer], 0.0)

    local_sweep(
        ((BLOCK,) * 4,) * 2, (BLOCK,) * 3, lambda count: 1,
        early_flag(flag_ref) * jnp.where(core == 0, 1.0, 0.0), u_ref, p_refs, c_ref, e_refs, rate_ref,
        weights, lanes, added, core == 0,
    )
    for k in range(BLOCK):
        out_ref[0, k] = e_refs[3][k + 1]
        for n in range(3):
            out_ref[n + 1, k] = e_refs[n][k + 1]


def block_kernel(flag_ref, w_ref, mixed_ref, swapped_ref, out_ref, *work):
    @pl.when(flag_ref[0] == 0)
    def _():
        own_ends(flag_ref, w_ref, mixed_ref, swapped_ref, out_ref, *work)


def respond(flag_ref, w_ref, sent_ref, got_ref, local_ref, base_ref, rest_ref, rate_ref, c_ref, work):
    core = flag_ref[1]
    p_refs, e_refs = work[:3], work[3:]
    weights, lanes = stacked_weights(w_ref), neighbour_lanes()
    flag = early_flag(flag_ref)
    for ref, reach in ((c_ref.at[0], 4), (e_refs[0], 5), (e_refs[1], 6), (e_refs[2], 7)):
        for k in range(BLOCK - reach):
            ref[k] = jnp.zeros(LAYER, F32)
            ref[2 * BLOCK - 1 - k] = jnp.zeros(LAYER, F32)
    for k in range(BLOCK):
        row = TRACES * FACE + k
        mine = jnp.broadcast_to(sent_ref[row : row + 1], (8, LANES))
        theirs = jnp.broadcast_to(got_ref[row : row + 1], (8, LANES))
        rate_ref[k] = jnp.where(core == 0, theirs, mine)
        rate_ref[BLOCK + k] = jnp.where(core == 0, mine, theirs)

    def step(reach, source, trace, store):
        start = BLOCK - reach
        mine, theirs = (r[trace * FACE : (trace + 1) * FACE] for r in (sent_ref, got_ref))

        def inject(k):
            if start + k == BLOCK - 1:
                return None, jnp.where(core == 0, mine, theirs)
            if start + k == BLOCK:
                return jnp.where(core == 0, theirs, mine), None
            return None, None

        def load(k):
            layer = start - 1 + k
            if not BLOCK - reach < layer < BLOCK + reach - 1:
                return jnp.zeros(LAYER, F32)
            return source(layer)

        sweep(
            2 * reach, load, lambda k: rate_ref[start + k], weights, lanes,
            lambda k, v, y: store(start + k, v, y), inject,
        )

    for power in range(4):
        for n in range(4):

            def source(layer, n=n, power=power):
                return p_refs[power - 1][n, layer]

            def store(layer, v, y, n=n, power=power):
                p = y - v
                if power < 3:
                    p_refs[power][n, layer] = p
                    return
                second = p_refs[1][n, layer] if BLOCK - 2 <= layer < BLOCK + 2 else 0.0
                more = None
                if n == 0 and BLOCK - 1 <= layer < BLOCK + 1:
                    more = flag * (STEP * p_refs[0][n, layer])
                c_ref[n, layer] = correction(second, v, p, more)

            step(power + 1, source, n * 4 + power, store)
    for n in range(3):

        def source(layer, n=n):
            return c_ref[0, layer] if n == 0 else e_refs[n - 1][layer]

        def store(layer, v, y, n=n):
            value = (1.0 - STEP) * v + STEP * y
            e_refs[n][layer] = value + c_ref[n + 1, layer] if BLOCK - 4 <= layer < BLOCK + 4 else value

        step(5 + n, source, 16 + n, store)

    side = jnp.where(core == 0, BLOCK, 0)
    for k in range(BLOCK):
        base_ref[0, k] = local_ref[0, k] + c_ref[0, side + k]
        for n in range(3):
            base_ref[n + 1, k] = local_ref[n + 1, k] + e_refs[n][side + k]
    for n in range(4):
        for x in range(4):
            rest_ref[n * 4 + x] = base_ref[n, 2 * x + 1 - core]


def early_kernel(flag_ref, w_ref, sent_ref, got_ref, local_ref, base_ref, last_ref, rest_ref, rate_ref, c_ref, *work):
    @pl.when(flag_ref[0] == 0)
    def _():
        respond(flag_ref, w_ref, sent_ref, got_ref, local_ref, base_ref, rest_ref, rate_ref, c_ref, work)
        for k in range(BLOCK):
            last_ref[k] = base_ref[3, k]


def join_kernel(flag_ref, w_ref, sent_ref, base_ref, last_ref, own_ref, out_ref, rate_ref, *e_refs):
    core = flag_ref[1]

    @pl.when(flag_ref[0] == 0)
    def _():
        weights, lanes = stacked_weights(w_ref), neighbour_lanes()
        for k in (0, BLOCK + 1):
            for ref in e_refs:
                ref[k] = jnp.zeros(LAYER, F32)
        for k in range(BLOCK):
            e_refs[0][k + 1] = base_ref[3, k] + last_ref[k]
            rate_ref[k + 1] = jnp.broadcast_to(sent_ref[TRACES * FACE + k : TRACES * FACE + k + 1], (8, LANES))
        for k in range(4):
            own_ref[k] = e_refs[0][1 + 4 * core + k]
        for n, count in enumerate((4, 2, 2)):
            start = jnp.where(core == 0, BLOCK + 1 - count, 1)

            def store(k, v, y, n=n, start=start):
                e_refs[n + 1][start + k] = (1.0 - STEP) * v + STEP * y

            sweep(
                count,
                lambda k, n=n, start=start: e_refs[n][start - 1 + k],
                lambda k, start=start: rate_ref[start + k],
                weights, lanes, store,
            )
        edge = jnp.where(core == 0, BLOCK, 1)
        for n in range(4):
            layer = e_refs[n][edge]
            out_ref[n * FACE : (n + 1) * FACE] = jnp.where(core == 0, layer[48:64], layer[0:16])


def late_kernel(
    flag_ref, w_ref, mixed_ref, swapped_ref, sent_ref, got_ref, rest_in_ref, base_ref, rest_ref, local_ref, *work
):
    @pl.when(flag_ref[0] == 1)
    def _():
        own_ends(flag_ref, w_ref, mixed_ref, swapped_ref, local_ref, *work[:10])
        respond(flag_ref, w_ref, sent_ref, got_ref, local_ref, base_ref, rest_ref, work[10], work[11], work[12:])

    @pl.when(flag_ref[0] == 0)
    def _():
        for k in range(16):
            rest_ref[k] = rest_in_ref[k]

    rest_ref[16, 0:BLOCK] = got_ref[TRACES * FACE :]


def finish_kernel(
    flag_ref, w_ref, sent_ref, got_ref, base_ref, late_base_ref, rest_ref,
    halo_ref, own_ref, halo_back_ref, own_back_ref, out_ref, rate_ref, start_ref, *e_refs,
):
    core = flag_ref[1]

    def row(ref, k):
        return jnp.broadcast_to(ref[k : k + 1], (8, LANES))

    @pl.when(flag_ref[0] == 1)
    def _():
        weights, lanes = stacked_weights(w_ref), neighbour_lanes()
        for k in range(4):
            start_ref[4 + k] = jnp.where(core == 0, own_ref[k], own_back_ref[k])
            start_ref[8 + k] = jnp.where(core == 0, own_back_ref[k], own_ref[k])
        for k in range(4):
            near, far = row(got_ref, TRACES * FACE + 4 + k), row(rest_ref.at[16], 4 + k)
            rate_ref[k] = jnp.where(core == 0, near, far)
            near, far = row(got_ref, TRACES * FACE + k), row(rest_ref.at[16], k)
            rate_ref[4 + BLOCK + k] = jnp.where(core == 0, far, near)
        for k in range(BLOCK):
            rate_ref[4 + k] = row(sent_ref, TRACES * FACE + k)
        for n in range(4):
            first = 1 + n
            source = start_ref if n == 0 else e_refs[n - 1]
            mine, theirs = (r[n * FACE : (n + 1) * FACE] for r in (halo_ref, halo_back_ref))
            sides = (jnp.where(core == 0, mine, theirs), jnp.where(core == 0, theirs, mine))

            def load(k, n=n, source=source, first=first):
                layer = first - 1 + k
                return source[layer] if 4 - n <= layer < 12 + n else jnp.zeros(LAYER, F32)

            def inject(k, first=first, sides=sides):
                return (sides[0] if first + k == 4 else None, sides[1] if first + k == 11 else None)

            def store(k, v, y, n=n, first=first):
                e_refs[n][first + k] = (1.0 - STEP) * v + STEP * y

            sweep(
                2 * BLOCK - 2 * first, load, lambda k, first=first: rate_ref[first + k],
                weights, lanes, store, inject,
            )
            for x in range(4):
                layer = 2 * x + core
                out_ref[n * 4 + x] = late_base_ref[n, layer] + rest_ref[n * 4 + x] + e_refs[n][4 + layer]

    @pl.when(flag_ref[0] == 0)
    def _():
        for n in range(4):
            for x in range(4):
                out_ref[n * 4 + x] = base_ref[n, 2 * x + core] + rest_ref[n * 4 + x]


def call(kernel, outs, scratch, n_in, flags=True):
    whole = pl.BlockSpec(memory_space=pltpu.VMEM)
    first = [pl.BlockSpec(memory_space=pltpu.SMEM)] if flags else []
    return pl.pallas_call(
        kernel,
        out_shape=tuple(jax.ShapeDtypeStruct(s, F32) for s in outs),
        in_specs=first + [whole] * (n_in - len(first)),
        out_specs=tuple(whole for _ in outs),
        scratch_shapes=[pltpu.VMEM(s, F32) for s in scratch],
        compiler_params=pltpu.CompilerParams(vmem_limit_bytes=VMEM),
    )


def leave(position, field):
    whole = pl.BlockSpec(memory_space=pltpu.VMEM)
    return pl.pallas_call(
        post_kernel,
        out_shape=jax.ShapeDtypeStruct((NODES * SOURCES, LANES), F32),
        in_specs=[whole] * 2,
        out_specs=pl.BlockSpec(memory_space=pltpu.HBM),
        scratch_shapes=[pltpu.VMEM((NODES * SOURCES, LANES), F32), pltpu.SemaphoreType.DMA((PARTS,))],
        compiler_params=pltpu.CompilerParams(vmem_limit_bytes=VMEM),
    )(position, field)


LAYER = (NODES, LANES)
RATES = (8, LANES)


def shards(slice_start, volume, lift_matrix, element_rate, position, neighbours):
    del neighbours
    zh, core = lax.axis_index("zh"), lax.axis_index("c")
    flags = jnp.stack([zh, core]).astype(jnp.int32)
    weights = jnp.dot(
        jnp.concatenate([volume, lift_matrix], axis=1), jnp.asarray(selection()), precision=lax.Precision.HIGHEST
    )
    row = position.reshape(1, LANES)
    (natural,) = call(pre_kernel, ((SOURCES, CHUNK, LANES),), (), 3, False)(
        row, element_rate.reshape(1, LANES), slice_start.reshape(NODES * SOURCES, LANES)
    )
    swap = [(0, 1), (1, 0)]
    mixed = lax.all_to_all(natural, ("y", "x"), 0, 0, tiled=True)
    swapped = lax.ppermute(mixed, "c", swap)

    def block_scratch(slices, corrections, ends):
        inner = BLOCK + 2
        return (
            (slices, inner) + LAYER, (inner,) + RATES, (corrections, inner) + LAYER,
            *[(slices, inner) + LAYER] * 3, *[(inner,) + LAYER] * ends,
        )

    (sent,) = call(edge_kernel, ((TRACES * FACE + 8, LANES),), block_scratch(4, 3, 2), 4)(flags, weights, mixed, swapped)
    axes = ("zh", "zl", "c")

    def meet(half):
        first = half * 4
        return [((first + z) * 2 + c, (first + (z + (-1, 1)[c]) % 4) * 2 + 1 - c) for z in range(4) for c in range(2)]

    got = lax.ppermute(sent, axes, meet(0))
    (local,) = call(block_kernel, ((4, BLOCK) + LAYER,), block_scratch(2, 2, 4), 4)(flags, weights, mixed, swapped)
    both = 2 * BLOCK
    scratch = ((both,) + RATES, *[(4, both) + LAYER] * 4, *[(both,) + LAYER] * 3)
    base, last, rest = call(
        early_kernel, ((4, BLOCK) + LAYER, (BLOCK,) + LAYER, (16,) + LAYER), scratch, 5
    )(flags, weights, sent, got, local)
    last = lax.ppermute(last, "c", swap)

    own_half, faces = call(
        join_kernel, ((4,) + LAYER, (4 * FACE, LANES)), ((BLOCK + 2,) + RATES, *[(BLOCK + 2,) + LAYER] * 4), 5
    )(flags, weights, sent, base, last)
    own_half, faces, rest, late_sent = lax.optimization_barrier((own_half, faces, rest, sent))
    straight = [(z * 2 + c, (4 + z) * 2 + c) for z in range(4) for c in range(2)]
    beside = [(z * 2 + c, (4 + (z + (1, -1)[c]) % 4) * 2 + c) for z in range(4) for c in range(2)]
    own = lax.ppermute(own_half, axes, straight)
    halo = lax.ppermute(faces, axes, beside)
    got = lax.ppermute(late_sent, axes, meet(1))
    late_base, rest = call(
        late_kernel,
        ((4, BLOCK) + LAYER, (17,) + LAYER),
        ((4, BLOCK) + LAYER, *block_scratch(2, 2, 4), *scratch),
        7,
    )(flags, weights, mixed, swapped, sent, got, rest)
    halo, own, rest = lax.optimization_barrier((halo, own, rest))
    rest = lax.ppermute(rest, "c", swap)
    (out,) = call(
        finish_kernel,
        ((SOURCES,) + LAYER,),
        ((both,) + RATES, (both,) + LAYER, *[(both,) + LAYER] * 4),
        11,
    )(
        flags, weights, sent, got, base, late_base, rest,
        halo, own, lax.ppermute(halo, "c", swap), lax.ppermute(own, "c", swap),
    )
    home = lax.all_to_all(out, ("y", "x"), 0, 0, tiled=True)
    return leave(row, home).reshape(slice_start.shape)


def solution(mesh):
    fine_mesh = Mesh(mesh.devices.reshape(2, 4, 4, 4, 2), ("zh", "y", "zl", "x", "c"))
    tm, space = ("zh", "y"), ("zl", "x", "c")
    placed = (P(tm, None, None, space), P(), P(), P(space), P(space), P(None, space))
    return jax.shard_map(
        shards, mesh=fine_mesh, in_specs=placed, out_specs=P(tm, None, None, space), check_vma=False
    )
```

```python
import functools

import jax
import jax.numpy as jnp
import numpy as np
from jax import lax
from jax.experimental import pallas as pl
from jax.experimental.pallas import tpu as pltpu
from jax.sharding import Mesh, PartitionSpec as P

STEP = 0.25
NODES = 64
LANES = 128
SOURCES = 16
COLS = 16
BLOCK = 8
CHUNK = 72
TRACES = 19
FACE = 16
RANK = 160
VMEM = 40 * 1024 * 1024
F32 = jnp.float32


def selection():
    table = np.zeros((160, RANK), np.float32)
    for a in range(4):
        for b in range(4):
            for c in range(4):
                node = a * 16 + b * 4 + c
                table[node, node] += 1.0
                faces = ((a, 0, b * 4 + c), (b, 2, a * 4 + c), (c, 4, a * 4 + b))
                for place, low, rank in faces:
                    if place == 0:
                        table[64 + low * 16 + rank, node] -= 1.0
                    if place == 3:
                        table[64 + (low + 1) * 16 + rank, node] -= 1.0
                place = 128 + a * 8 + (node % 8 + (2 if node % 16 >= 8 else 0)) % 8
                if c == 0:
                    table[64 + 5 * 16 + a * 4 + b, place] = 1.0
                if c == 3:
                    table[64 + 4 * 16 + a * 4 + b, place] = 1.0
    for k in range(16):
        table[64 + k, 64 + k] = 1.0
        table[64 + 16 + k, 80 + k] = 1.0
    for a in range(4):
        for c in range(4):
            table[64 + 3 * 16 + a * 4 + c, 96 + a * 8 + c] = 1.0
            table[64 + 2 * 16 + a * 4 + c, 96 + a * 8 + 4 + c] = 1.0
    return table


def gather_lanes(x, index):
    return jnp.take_along_axis(x, index, axis=1, mode="promise_in_bounds")


def neighbour_lanes():
    lane = lax.broadcasted_iota(jnp.int32, (8, LANES), 1)
    row = lax.broadcasted_iota(jnp.int32, (8, LANES), 0)
    y_index = jnp.where(row < 4, lane + COLS, lane + (LANES - COLS)) & (LANES - 1)
    col = lane & (COLS - 1)
    z_step = jnp.where((row & 1) == 0, 1, COLS - 1)
    z_index = (lane - col) + ((col + z_step) & (COLS - 1))
    return y_index, z_index, row < 4, ((row + 1) & 3) < 2


def operand(before, here, after, lanes):
    y_index, z_index, low, outer = lanes
    ys = [
        gather_lanes(jnp.where(low, here[16 * a : 16 * a + 8], here[16 * a + 8 : 16 * a + 16]), y_index)
        for a in range(4)
    ]
    zs = [
        gather_lanes(
            jnp.where(outer, here[16 * a : 16 * a + 8], pltpu.roll(here[16 * a + 8 : 16 * a + 16], 2, 0)), z_index
        )
        for a in range(4)
    ]
    return jnp.concatenate([here, before, after] + ys + zs, axis=0)


def split(x):
    high = x.astype(jnp.bfloat16)
    low = (x - high.astype(F32)).astype(jnp.bfloat16)
    return high, low


def product(weights, x):
    high, low = split(x)
    first = jnp.dot(weights, high, preferred_element_type=F32)
    second = jnp.dot(weights[:NODES], low, preferred_element_type=F32)
    return first[:NODES] + first[NODES:] + second


def stacked_weights(w_ref):
    high, low = split(w_ref[...])
    return jnp.concatenate([high, low], axis=0)


def sweep(count, load, rates, weights, lanes, store, inject=None):
    for k in range(0, count, 2):
        v = [load(k + i) for i in range(4)]
        x = []
        for i in range(2):
            before, after = v[i][48:64], v[i + 2][0:16]
            extra = inject(k + i) if inject is not None else (None, None)
            before = before if extra[0] is None else before + extra[0]
            after = after if extra[1] is None else after + extra[1]
            x.append(operand(before, v[i + 1], after, lanes))
        y = product(weights, jnp.concatenate(x, axis=1))
        for i in range(2):
            rate = jnp.concatenate([rates(k + i)] * (NODES // 8), axis=0)
            store(k + i, v[i + 1], rate * y[:, i * LANES : (i + 1) * LANES])


def slot_row(position):
    where = lax.broadcasted_iota(jnp.int32, (LANES, LANES), 0)
    hit = jnp.where(position == where, 1.0, 0.0).astype(jnp.bfloat16)
    ids = lax.broadcasted_iota(jnp.int32, (16, LANES), 1).astype(F32).astype(jnp.bfloat16)
    found = lax.dot_general(ids, hit, (((1,), (1,)), ((), ())), preferred_element_type=F32)
    return found[0:1].astype(jnp.int32)


PARTS = 4
PART_NODES = NODES // PARTS
PART_ROWS = PART_NODES * SOURCES


def pre_kernel(position_ref, rate_ref, field_ref, out_ref):
    index = jnp.broadcast_to(slot_row(position_ref[...]), (NODES, LANES))
    rate = gather_lanes(jnp.broadcast_to(rate_ref[...], (8, LANES)), index[:8])
    for s in range(SOURCES):
        out_ref[s, 0:NODES] = gather_lanes(field_ref[pl.ds(s, NODES, stride=SOURCES), :], index)
        out_ref[s, NODES:CHUNK] = rate


def post_kernel(position_ref, field_ref, out_hbm, out_ref, sems):
    index = jnp.broadcast_to(position_ref[...], (PART_NODES, LANES))
    copies = []
    for part in range(PARTS):
        for s in range(SOURCES):
            piece = gather_lanes(field_ref[s, part * PART_NODES : (part + 1) * PART_NODES], index)
            out_ref[pl.ds(part * PART_ROWS + s, PART_NODES, stride=SOURCES), :] = piece
        rows = pl.ds(part * PART_ROWS, PART_ROWS)
        copies.append(pltpu.make_async_copy(out_ref.at[rows], out_hbm.at[rows], sems.at[part]))
        copies[-1].start()
    for copy in copies:
        copy.wait()


def fill_block(core, mixed_ref, swapped_ref, u_ref, rate_ref, slices=range(4)):
    for n, which in enumerate(slices):
        for k in range(BLOCK):
            chunk = which * 4 + k // 2
            u_ref[n, k + 1] = jnp.where(core == k % 2, mixed_ref[chunk, 0:NODES], swapped_ref[chunk, 0:NODES])
    for k in range(BLOCK):
        rate_ref[k + 1] = jnp.where(
            core == k % 2, mixed_ref[k // 2, NODES:CHUNK], swapped_ref[k // 2, NODES:CHUNK]
        )


def local_sweep(counts, ends, first, flag, u_ref, p_refs, c_ref, e_refs, rate_ref, weights, lanes, added, has_first=None):
    for power in range(4):
        source = u_ref if power == 0 else p_refs[power - 1]
        for n, powers in enumerate(counts):
            if power >= len(powers):
                continue
            start = first(powers[power])

            def load(k, source=source, start=start, n=n):
                return source[n, start - 1 + k]

            def rates(k, start=start):
                return rate_ref[start + k]

            def store(k, v, y, n=n, power=power, start=start):
                p = y - v
                if power < 3:
                    p_refs[power][n, start + k] = p
                else:
                    c_ref[n, start + k] = correction(
                        p_refs[1][n, start + k], v, p,
                        flag * (u_ref[n, start + k] + STEP * p_refs[0][n, start + k]) if n == 0 else None,
                    )

            sweep(powers[power], load, rates, weights, lanes, store)
    if has_first is not None:
        for k in range(BLOCK + 2):
            e_refs[3][k] = jnp.where(has_first, c_ref[0, k], 0.0)
    for n, count in enumerate(ends):
        source = e_refs[n - 1] if n else c_ref.at[0] if has_first is None else e_refs[3]
        start = first(count)

        def load(k, source=source, start=start):
            return source[start - 1 + k]

        def rates(k, start=start):
            return rate_ref[start + k]

        def store(k, v, y, n=n, start=start):
            e_refs[n][start + k] = (1.0 - STEP) * v + STEP * y + added(n + 1, start + k)

        sweep(count, load, rates, weights, lanes, store)


def clear_sides(u_ref, p_refs, c_ref, e_refs):
    for k in (0, BLOCK + 1):
        for ref in (u_ref, *p_refs, c_ref):
            for n in range(ref.shape[0]):
                ref[n, k] = jnp.zeros(LAYER, F32)
        for ref in e_refs:
            ref[k] = jnp.zeros(LAYER, F32)


def correction(second, third, fourth, more=None):
    total = (STEP**2 / 2) * second + (STEP**3 / 6) * third + (STEP**4 / 24) * fourth
    return total if more is None else total + more


def early_flag(flag_ref):
    return jnp.where(flag_ref[0] == 0, 1.0, 0.0).astype(F32)


def edge_kernel(flag_ref, w_ref, mixed_ref, swapped_ref, out_ref, u_ref, rate_ref, c_ref, *work):
    core = flag_ref[1]
    p_refs, e_refs = work[:3], work[3:]
    weights, lanes = stacked_weights(w_ref), neighbour_lanes()
    fill_block(core, mixed_ref, swapped_ref, u_ref, rate_ref)
    clear_sides(u_ref, p_refs, c_ref, e_refs)
    local_sweep(
        ((6, 6, 4, 4), (6, 4, 4, 2), (4, 4, 2, 2), (4, 2, 2)),
        (2, 2),
        lambda count: jnp.where(core == 0, 1, BLOCK + 1 - count),
        early_flag(flag_ref), u_ref, p_refs, c_ref, e_refs, rate_ref, weights, lanes,
        lambda n, layer: c_ref[n, layer],
    )
    edge = jnp.where(core == 0, 1, BLOCK)
    for t in range(TRACES):
        n, power = t // 4, t % 4
        if t < 16:
            layer = u_ref[n, edge] if power == 0 else p_refs[power - 1][n, edge]
        else:
            layer = c_ref[0, edge] if t == 16 else e_refs[t - 17][edge]
        out_ref[t * FACE : (t + 1) * FACE] = jnp.where(core == 0, layer[0:16], layer[48:64])
    out_ref[TRACES * FACE :] = jnp.concatenate([rate_ref[k + 1, 0:1] for k in range(BLOCK)], axis=0)


def own_ends(flag_ref, w_ref, mixed_ref, swapped_ref, out_ref, u_ref, rate_ref, c_ref, *work):
    core = flag_ref[1]
    p_refs, e_refs = work[:3], work[3:]
    weights, lanes = stacked_weights(w_ref), neighbour_lanes()
    fill_block(core, mixed_ref, swapped_ref, u_ref, rate_ref, (core, 3 - core))
    clear_sides(u_ref, p_refs, c_ref, e_refs)

    def added(n, layer):
        return jnp.where(core == (0 if n == 3 else 1), c_ref[1 if n > 1 else 0, layer], 0.0)

    local_sweep(
        ((BLOCK,) * 4,) * 2, (BLOCK,) * 3, lambda count: 1,
        early_flag(flag_ref) * jnp.where(core == 0, 1.0, 0.0), u_ref, p_refs, c_ref, e_refs, rate_ref,
        weights, lanes, added, core == 0,
    )
    for k in range(BLOCK):
        out_ref[0, k] = e_refs[3][k + 1]
        for n in range(3):
            out_ref[n + 1, k] = e_refs[n][k + 1]


def block_kernel(flag_ref, w_ref, mixed_ref, swapped_ref, out_ref, *work):
    @pl.when(flag_ref[0] == 0)
    def _():
        own_ends(flag_ref, w_ref, mixed_ref, swapped_ref, out_ref, *work)


def respond(flag_ref, w_ref, sent_ref, got_ref, local_ref, base_ref, rest_ref, rate_ref, c_ref, work):
    core = flag_ref[1]
    p_refs, e_refs = work[:3], work[3:]
    weights, lanes = stacked_weights(w_ref), neighbour_lanes()
    flag = early_flag(flag_ref)
    for ref, reach in (*((c_ref.at[n], 4) for n in range(4)), (e_refs[0], 5), (e_refs[1], 6), (e_refs[2], 7)):
        for k in range(BLOCK - reach):
            ref[k] = jnp.zeros(LAYER, F32)
            ref[2 * BLOCK - 1 - k] = jnp.zeros(LAYER, F32)
    for k in range(BLOCK):
        row = TRACES * FACE + k
        mine = jnp.broadcast_to(sent_ref[row : row + 1], (8, LANES))
        theirs = jnp.broadcast_to(got_ref[row : row + 1], (8, LANES))
        rate_ref[k] = jnp.where(core == 0, theirs, mine)
        rate_ref[BLOCK + k] = jnp.where(core == 0, mine, theirs)

    def step(reach, source, trace, store):
        start = BLOCK - reach
        mine, theirs = (r[trace * FACE : (trace + 1) * FACE] for r in (sent_ref, got_ref))

        def inject(k):
            if start + k == BLOCK - 1:
                return None, jnp.where(core == 0, mine, theirs)
            if start + k == BLOCK:
                return jnp.where(core == 0, theirs, mine), None
            return None, None

        def load(k):
            layer = start - 1 + k
            if not BLOCK - reach < layer < BLOCK + reach - 1:
                return jnp.zeros(LAYER, F32)
            return source(layer)

        sweep(
            2 * reach, load, lambda k: rate_ref[start + k], weights, lanes,
            lambda k, v, y: store(start + k, v, y), inject,
        )

    for power in range(4):
        for n in range(4):

            def source(layer, n=n, power=power):
                return p_refs[power - 1][n, layer]

            def store(layer, v, y, n=n, power=power):
                p = y - v
                if power < 3:
                    p_refs[power][n, layer] = p
                    return
                second = p_refs[1][n, layer] if BLOCK - 2 <= layer < BLOCK + 2 else 0.0
                more = None
                if n == 0 and BLOCK - 1 <= layer < BLOCK + 1:
                    more = flag * (STEP * p_refs[0][n, layer])
                c_ref[n, layer] = correction(second, v, p, more)

            step(power + 1, source, n * 4 + power, store)
    for n in range(3):
        reach, beyond = 5 + n, 3 - n
        start = jnp.where(core == 0, BLOCK - beyond, BLOCK - reach)
        source = c_ref.at[0] if n == 0 else e_refs[n - 1]
        trace = 16 + n
        mine, theirs = (r[trace * FACE : (trace + 1) * FACE] for r in (sent_ref, got_ref))
        faces = {
            beyond: (jnp.where(core == 0, theirs, 0.0), None),
            beyond - 1: (None, jnp.where(core == 0, mine, 0.0)),
            reach: (jnp.where(core == 0, 0.0, mine), None),
            reach - 1: (None, jnp.where(core == 0, 0.0, theirs)),
        }

        def store(k, v, y, n=n, start=start):
            e_refs[n][start + k] = (1.0 - STEP) * v + STEP * y + c_ref[n + 1, start + k]

        sweep(
            reach + beyond,
            lambda k, source=source, start=start: source[start - 1 + k],
            lambda k, start=start: rate_ref[start + k],
            weights, lanes, store,
            lambda k, faces=faces: faces.get(k, (None, None)),
        )

    side = jnp.where(core == 0, BLOCK, 0)
    for k in range(BLOCK):
        base_ref[0, k] = local_ref[0, k] + c_ref[0, side + k]
        for n in range(3):
            base_ref[n + 1, k] = local_ref[n + 1, k] + e_refs[n][side + k]
    for n in range(4):
        for x in range(4):
            rest_ref[n * 4 + x] = base_ref[n, 2 * x + 1 - core]


def early_kernel(flag_ref, w_ref, sent_ref, got_ref, local_ref, base_ref, last_ref, rest_ref, rate_ref, c_ref, *work):
    @pl.when(flag_ref[0] == 0)
    def _():
        respond(flag_ref, w_ref, sent_ref, got_ref, local_ref, base_ref, rest_ref, rate_ref, c_ref, work)
        for k in range(BLOCK):
            last_ref[k] = base_ref[3, k]


def join_kernel(flag_ref, w_ref, sent_ref, base_ref, last_ref, own_ref, out_ref, rate_ref, *e_refs):
    core = flag_ref[1]

    @pl.when(flag_ref[0] == 0)
    def _():
        weights, lanes = stacked_weights(w_ref), neighbour_lanes()
        for k in (0, BLOCK + 1):
            for ref in e_refs:
                ref[k] = jnp.zeros(LAYER, F32)
        for k in range(BLOCK):
            e_refs[0][k + 1] = base_ref[3, k] + last_ref[k]
            rate_ref[k + 1] = jnp.broadcast_to(sent_ref[TRACES * FACE + k : TRACES * FACE + k + 1], (8, LANES))
        for k in range(4):
            own_ref[k] = e_refs[0][1 + 4 * core + k]
        for n, count in enumerate((4, 2, 2)):
            start = jnp.where(core == 0, BLOCK + 1 - count, 1)

            def store(k, v, y, n=n, start=start):
                e_refs[n + 1][start + k] = (1.0 - STEP) * v + STEP * y

            sweep(
                count,
                lambda k, n=n, start=start: e_refs[n][start - 1 + k],
                lambda k, start=start: rate_ref[start + k],
                weights, lanes, store,
            )
        edge = jnp.where(core == 0, BLOCK, 1)
        for n in range(4):
            layer = e_refs[n][edge]
            out_ref[n * FACE : (n + 1) * FACE] = jnp.where(core == 0, layer[48:64], layer[0:16])


def late_kernel(
    flag_ref, w_ref, mixed_ref, swapped_ref, sent_ref, got_ref, rest_in_ref, base_ref, rest_ref, local_ref, *work
):
    @pl.when(flag_ref[0] == 1)
    def _():
        own_ends(flag_ref, w_ref, mixed_ref, swapped_ref, local_ref, *work[:10])
        respond(flag_ref, w_ref, sent_ref, got_ref, local_ref, base_ref, rest_ref, work[10], work[11], work[12:])

    @pl.when(flag_ref[0] == 0)
    def _():
        for k in range(16):
            rest_ref[k] = rest_in_ref[k]

    rest_ref[16, 0:BLOCK] = got_ref[TRACES * FACE :]


def finish_kernel(
    flag_ref, w_ref, sent_ref, got_ref, base_ref, late_base_ref, rest_ref,
    halo_ref, own_ref, halo_back_ref, own_back_ref, out_ref, rate_ref, start_ref, *e_refs,
):
    core = flag_ref[1]

    def row(ref, k):
        return jnp.broadcast_to(ref[k : k + 1], (8, LANES))

    @pl.when(flag_ref[0] == 1)
    def _():
        weights, lanes = stacked_weights(w_ref), neighbour_lanes()
        for k in range(4):
            start_ref[4 + k] = jnp.where(core == 0, own_ref[k], own_back_ref[k])
            start_ref[8 + k] = jnp.where(core == 0, own_back_ref[k], own_ref[k])
        for k in range(4):
            near, far = row(got_ref, TRACES * FACE + 4 + k), row(rest_ref.at[16], 4 + k)
            rate_ref[k] = jnp.where(core == 0, near, far)
            near, far = row(got_ref, TRACES * FACE + k), row(rest_ref.at[16], k)
            rate_ref[4 + BLOCK + k] = jnp.where(core == 0, far, near)
        for k in range(BLOCK):
            rate_ref[4 + k] = row(sent_ref, TRACES * FACE + k)
        for n in range(4):
            first = 1 + n
            source = start_ref if n == 0 else e_refs[n - 1]
            mine, theirs = (r[n * FACE : (n + 1) * FACE] for r in (halo_ref, halo_back_ref))
            sides = (jnp.where(core == 0, mine, theirs), jnp.where(core == 0, theirs, mine))

            def load(k, n=n, source=source, first=first):
                layer = first - 1 + k
                return source[layer] if 4 - n <= layer < 12 + n else jnp.zeros(LAYER, F32)

            def inject(k, first=first, sides=sides):
                return (sides[0] if first + k == 4 else None, sides[1] if first + k == 11 else None)

            def store(k, v, y, n=n, first=first):
                e_refs[n][first + k] = (1.0 - STEP) * v + STEP * y

            sweep(
                2 * BLOCK - 2 * first, load, lambda k, first=first: rate_ref[first + k],
                weights, lanes, store, inject,
            )
            for x in range(4):
                layer = 2 * x + core
                out_ref[n * 4 + x] = late_base_ref[n, layer] + rest_ref[n * 4 + x] + e_refs[n][4 + layer]

    @pl.when(flag_ref[0] == 0)
    def _():
        for n in range(4):
            for x in range(4):
                out_ref[n * 4 + x] = base_ref[n, 2 * x + core] + rest_ref[n * 4 + x]


def call(kernel, outs, scratch, n_in, flags=True):
    whole = pl.BlockSpec(memory_space=pltpu.VMEM)
    first = [pl.BlockSpec(memory_space=pltpu.SMEM)] if flags else []
    return pl.pallas_call(
        kernel,
        out_shape=tuple(jax.ShapeDtypeStruct(s, F32) for s in outs),
        in_specs=first + [whole] * (n_in - len(first)),
        out_specs=tuple(whole for _ in outs),
        scratch_shapes=[pltpu.VMEM(s, F32) for s in scratch],
        compiler_params=pltpu.CompilerParams(vmem_limit_bytes=VMEM),
    )


def leave(position, field):
    whole = pl.BlockSpec(memory_space=pltpu.VMEM)
    return pl.pallas_call(
        post_kernel,
        out_shape=jax.ShapeDtypeStruct((NODES * SOURCES, LANES), F32),
        in_specs=[whole] * 2,
        out_specs=pl.BlockSpec(memory_space=pltpu.HBM),
        scratch_shapes=[pltpu.VMEM((NODES * SOURCES, LANES), F32), pltpu.SemaphoreType.DMA((PARTS,))],
        compiler_params=pltpu.CompilerParams(vmem_limit_bytes=VMEM),
    )(position, field)


LAYER = (NODES, LANES)
RATES = (8, LANES)


def shards(slice_start, volume, lift_matrix, element_rate, position, neighbours):
    del neighbours
    zh, core = lax.axis_index("zh"), lax.axis_index("c")
    flags = jnp.stack([zh, core]).astype(jnp.int32)
    weights = jnp.dot(
        jnp.concatenate([volume, lift_matrix], axis=1), jnp.asarray(selection()), precision=lax.Precision.HIGHEST
    )
    row = position.reshape(1, LANES)
    (natural,) = call(pre_kernel, ((SOURCES, CHUNK, LANES),), (), 3, False)(
        row, element_rate.reshape(1, LANES), slice_start.reshape(NODES * SOURCES, LANES)
    )
    swap = [(0, 1), (1, 0)]
    mixed = lax.all_to_all(natural, ("y", "x"), 0, 0, tiled=True)
    swapped = lax.ppermute(mixed, "c", swap)

    def block_scratch(slices, corrections, ends):
        inner = BLOCK + 2
        return (
            (slices, inner) + LAYER, (inner,) + RATES, (corrections, inner) + LAYER,
            *[(slices, inner) + LAYER] * 3, *[(inner,) + LAYER] * ends,
        )

    (sent,) = call(edge_kernel, ((TRACES * FACE + 8, LANES),), block_scratch(4, 3, 2), 4)(flags, weights, mixed, swapped)
    axes = ("zh", "zl", "c")

    def meet(half):
        first = half * 4
        return [((first + z) * 2 + c, (first + (z + (-1, 1)[c]) % 4) * 2 + 1 - c) for z in range(4) for c in range(2)]

    got = lax.ppermute(sent, axes, meet(0))
    (local,) = call(block_kernel, ((4, BLOCK) + LAYER,), block_scratch(2, 2, 4), 4)(flags, weights, mixed, swapped)
    both = 2 * BLOCK
    scratch = ((both,) + RATES, *[(4, both) + LAYER] * 4, *[(both,) + LAYER] * 3)
    base, last, rest = call(
        early_kernel, ((4, BLOCK) + LAYER, (BLOCK,) + LAYER, (16,) + LAYER), scratch, 5
    )(flags, weights, sent, got, local)
    last = lax.ppermute(last, "c", swap)

    own_half, faces = call(
        join_kernel, ((4,) + LAYER, (4 * FACE, LANES)), ((BLOCK + 2,) + RATES, *[(BLOCK + 2,) + LAYER] * 4), 5
    )(flags, weights, sent, base, last)
    own_half, faces, rest, late_sent = lax.optimization_barrier((own_half, faces, rest, sent))
    straight = [(z * 2 + c, (4 + z) * 2 + c) for z in range(4) for c in range(2)]
    beside = [(z * 2 + c, (4 + (z + (1, -1)[c]) % 4) * 2 + c) for z in range(4) for c in range(2)]
    own = lax.ppermute(own_half, axes, straight)
    halo = lax.ppermute(faces, axes, beside)
    got = lax.ppermute(late_sent, axes, meet(1) + [(i, i) for i in range(8)])
    late_base, rest = call(
        late_kernel,
        ((4, BLOCK) + LAYER, (17,) + LAYER),
        ((4, BLOCK) + LAYER, *block_scratch(2, 2, 4), *scratch),
        7,
    )(flags, weights, mixed, swapped, sent, got, rest)
    halo, own, rest = lax.optimization_barrier((halo, own, rest))
    rest = lax.ppermute(rest, "c", swap)
    (out,) = call(
        finish_kernel,
        ((SOURCES,) + LAYER,),
        ((both,) + RATES, (both,) + LAYER, *[(both,) + LAYER] * 4),
        11,
    )(
        flags, weights, sent, got, base, late_base, rest,
        halo, own, lax.ppermute(halo, "c", swap), lax.ppermute(own, "c", swap),
    )
    home = lax.all_to_all(out, ("y", "x"), 0, 0, tiled=True)
    return leave(row, home).reshape(slice_start.shape)


def solution(mesh):
    fine_mesh = Mesh(mesh.devices.reshape(2, 4, 4, 4, 2), ("zh", "y", "zl", "x", "c"))
    tm, space = ("zh", "y"), ("zl", "x", "c")
    placed = (P(tm, None, None, space), P(), P(), P(space), P(space), P(None, space))
    return jax.shard_map(
        shards, mesh=fine_mesh, in_specs=placed, out_specs=P(tm, None, None, space), check_vma=False
    )
```
